128 devices in a mesh: front: 8 (over z, core), grid: 16 (over x, y).
Axes of the slice: x: 4, y: 4, z: 4, core: 2. Of those that a mesh axis runs over, the one named last changes fastest.
Arguments:
- front_entries: float32 [8, 2, 16, 128, 4096], P('front', None, 'grid'), may hold values from -1 to 2.5, as said below
- child_tiles: float32 [8, 2048, 128, 128], P('front', 'grid'), may hold values from -6 to 6
- tile_owner: int32 [8, 2048, 1], P('front', 'grid'), may hold values from 0 to 127; in each aligned block of 128 rows (0 to 127, 128 to 255, ..., all dimensions but the last counted through in order) at most 2 rows name the same one
- tile_rows: int32 [8, 2048], P('front', 'grid'), may hold values from 0 to 1
- tile_picks: int32 [8, 2048], P('front', 'grid'), may hold values from 0 to 31
Outputs:
- factored: float32 [8, 2, 16, 128, 4096], P('front', None, 'grid')
The draws below stay inside these ranges and needn't reach their ends.
Inputs may be any that keep to these rules, and one draw needn't show every extreme that they name: `tile_owner`: destination device is front index * 16 + grid index. Each device sends at most 2 of its tiles to any one device, and some device sends exactly 2 to one device. `front_entries`: entries above each front's diagonal are zero; the leading 2 * 512 rows and columns of each front form a positive definite block.
All inputs are finite; a program needn't handle non-finite values.
Results may differ from the reference program's by a relative error of at most 0.0001.
Values sent between devices are 32-bit elements; how exact they have to be, the bound alone decides.
No kernel may reach another device: no remote copies, remote signals or barrier semaphores. Data moves between devices by JAX's collectives and lax.ppermute only.
A program may use at most 192 MiB of HBM per device.

```python
import math
import jax
import jax.numpy as jnp
import numpy as np
from jax import lax

F = 4096
BLOCK = 128
PANEL = 512
PANELS = 2
CT = 128
CAP = 2
RBLOCKS = 2
FBLOCKS = 32
N_FRONT = 8
N_GRID = 16
DEVICES = 128


def draw_front_entries(key, part):
    key = jax.random.fold_in(key, 11)
    subkeys = jax.random.split(key, 2)
    full_shape = (N_FRONT, F // (BLOCK * N_GRID), N_GRID, BLOCK, F)
    lead_rows = PANELS * PANEL
    lead_scale = 0.5 / math.sqrt(lead_rows)
    blocks = lax.broadcasted_iota(jnp.int32, full_shape, 1) * N_GRID + lax.broadcasted_iota(jnp.int32, full_shape, 2)
    row_index = blocks * BLOCK + lax.broadcasted_iota(jnp.int32, full_shape, 3)
    col_index = lax.broadcasted_iota(jnp.int32, full_shape, 4)
    rough_part = jnp.clip(0.6 * jax.random.normal(subkeys[0], full_shape, jnp.float32), -1.0, 1.0)
    pivots = jax.random.uniform(subkeys[1], full_shape, jnp.float32, 1.25, 2.5)
    entries = jnp.where(row_index < lead_rows, lead_scale * rough_part, jnp.where(col_index < lead_rows, 0.25 * rough_part, rough_part))
    entries = jnp.where(row_index == col_index, jnp.where(row_index < lead_rows, pivots, rough_part), entries)
    return jnp.where(col_index <= row_index, entries, 0.0)


def touch_ends(result, stream_key, least, largest):
    longest = result.shape.index(max(result.shape))
    spots = []
    for shift in (0, 1):
        where = [jax.random.randint(jax.random.fold_in(stream_key, axis), (), 0, length) for axis, length in enumerate(result.shape)]
        where[longest] = (where[longest] + shift) % result.shape[longest]
        spots.append(tuple(where))
    return result.at[spots[0]].set(least).at[spots[1]].set(largest)


def level_of(stream_key, shape, cuts, low, high):
    loudness = 1.0
    for dim, blocks in cuts:
        heights = jax.random.uniform(jax.random.fold_in(jax.random.fold_in(stream_key, 6), dim), (blocks,), jnp.float32, low / len(cuts), high / len(cuts))
        loudness = loudness * jnp.repeat(jnp.exp(heights), shape[dim] // blocks).reshape((-1,) + (1,) * (len(shape) - 1 - dim))
    return loudness


def deal_out(own_key, own, number, rows, count, top, bound, slope):
    sequence = jax.random.permutation(own_key, count)
    heavy_load, common = portions_of(count, rows * top, bound, slope, True), portions_of(count, rows * top, bound, slope, False)
    places = jnp.arange(count)

    def named(lengths, offset_by):
        used = int((lengths > 0).sum())
        fixed = max(1, used // 4)
        moved = fixed + (places - fixed + offset_by * (used - fixed)) % max(1, count - fixed)
        return jnp.zeros((count,), jnp.int32).at[sequence[jnp.where(places < fixed, places, moved)]].set(jnp.asarray(lengths, jnp.int32))

    lengths = jnp.where(number % 4 == 0, named(heavy_load, number // 4), named(common, number - number // 4 - 1))
    mixed = jax.random.permutation(jax.random.fold_in(own, 3), count)
    source_of, taker = mixed[0:count // 2 * 2:2], mixed[1:count // 2 * 2:2]
    margin = jnp.minimum(lengths[source_of] - 1, bound - lengths[taker]) // 2
    margin = jnp.where((source_of == sequence[0]) | (taker == sequence[0]) | (lengths[taker] == 0), 0, jnp.maximum(margin, 0))
    moved = jax.random.randint(jax.random.fold_in(own, 4), (count // 2,), 0, 1 << 20) % (margin + 1)
    lengths = lengths.at[source_of].add(-moved).at[taker].add(moved)
    labels = jnp.searchsorted(jnp.cumsum(lengths), jnp.arange(rows * top), side="right").astype(jnp.int32)
    table = labels.reshape(top, rows).T
    table = table[jax.random.permutation(jax.random.fold_in(own, 1), rows)]
    offset_by = jax.random.randint(jax.random.fold_in(own, 2), (rows, 1), 0, top)
    return jnp.take_along_axis(table, (jnp.arange(top)[None, :] + offset_by) % top, axis=1)


def portions_of(count, total, reach, slope, full):
    weights = [(1 << 20) // math.isqrt(rank ** slope) + 1 for rank in range(1, count + 1)]
    largest = reach if full else min(reach, max(-(-total // count), total * weights[0] // sum(weights)))
    least = 1 if total - largest >= count - 1 else 0
    counts, rest = [largest] + [least] * (count - 1), total - largest - least * (count - 1)
    while rest > 0:
        candidates = [i for i in range(1, count) if counts[i] < largest] or [i for i in range(1, count) if counts[i] < reach]
        pool, left = sum([weights[i] for i in candidates]), rest
        for i in candidates:
            more = min(reach - counts[i], max(1, left * weights[i] // pool), rest)
            counts[i] = counts[i] + more
            rest = rest - more
    return np.array(counts)


def normal_values(own_key, dims, width, bound, cuts=(), kind=jnp.bfloat16):
    factor_of = level_of(own_key, dims, cuts, -0.22, 0.18) if cuts else 1.0
    drawn = jax.random.normal(own_key, dims, jnp.float32) * width * factor_of
    return jnp.minimum(jnp.maximum(drawn, -bound), bound).astype(kind)


def setup_inputs(seed: int = 0) -> dict:
    key_of = jax.random.split(jax.random.key(seed), 6)
    front_entries = draw_front_entries(jax.random.fold_in(key_of[5], 71), 0)
    child_tiles = normal_values(key_of[1], (N_FRONT, N_GRID * CT, BLOCK, BLOCK), 1.0, 6.0, ((0, 8), (1, 16)), jnp.float32)
    tile_owner_keys = jax.random.split(jax.random.fold_in(key_of[2], 1), N_FRONT * (N_GRID * CT) // CT)
    tile_owner_turns = jax.random.permutation(jax.random.fold_in(key_of[2], 3), N_FRONT * (N_GRID * CT) // CT)
    tile_owner = jax.vmap(lambda own, number: deal_out(jax.random.fold_in(key_of[2], 2), own, number, CT, DEVICES, 1, CAP, 2))(tile_owner_keys, tile_owner_turns).reshape((N_FRONT, N_GRID * CT, 1))
    tile_rows = touch_ends(jax.random.randint(key_of[3], (N_FRONT, N_GRID * CT), 0, RBLOCKS), jax.random.fold_in(key_of[3], 1), 0, RBLOCKS - 1).astype(jnp.int32)
    tile_picks = touch_ends(jax.random.randint(key_of[4], (N_FRONT, N_GRID * CT), 0, FBLOCKS), jax.random.fold_in(key_of[4], 1), 0, FBLOCKS - 1).astype(jnp.int32)
    return dict(front_entries=front_entries, child_tiles=child_tiles, tile_owner=tile_owner, tile_rows=tile_rows, tile_picks=tile_picks)


highest = lax.Precision.HIGHEST

def factor_block(block):
    symmetric = jnp.tril(block) + jnp.tril(block, -1).T
    return jnp.linalg.cholesky(symmetric)

def factor_front(front_matrix):
    for panel_step in range(PANELS):
        first_col = panel_step * PANEL
        last_col = first_col + PANEL
        factor = factor_block(front_matrix[first_col:last_col, first_col:last_col])
        below = front_matrix[last_col:, first_col:last_col]
        solved = jax.scipy.linalg.solve_triangular(factor, below.T, lower=True).T
        trailing = front_matrix[last_col:, last_col:] - jnp.dot(solved, solved.T, precision=highest)
        front_matrix = front_matrix.at[first_col:last_col, first_col:last_col].set(factor)
        front_matrix = front_matrix.at[last_col:, first_col:last_col].set(solved)
        front_matrix = front_matrix.at[last_col:, last_col:].set(jnp.tril(trailing))
    return front_matrix

def reference(front_entries, child_tiles, tile_owner, tile_rows, tile_picks):
    lead_blocks = PANELS * PANEL // BLOCK
    owners = tile_owner.reshape(-1).astype(jnp.int32)
    local_rows = tile_rows.reshape(-1).astype(jnp.int32)
    picks = tile_picks.reshape(-1).astype(jnp.int32)
    target_front = owners // N_GRID
    position = owners % N_GRID
    shifted = local_rows + (local_rows * N_GRID + position < lead_blocks).astype(jnp.int32)
    row_block = shifted * N_GRID + position
    col_block = picks % (row_block + 1)
    tile_data = child_tiles.reshape(-1, BLOCK, BLOCK)
    extra = jnp.zeros((N_FRONT, F // BLOCK, BLOCK, F // BLOCK, BLOCK), jnp.float32)
    extra = extra.at[target_front, row_block, :, col_block, :].add(tile_data)
    assembled = jnp.tril(front_entries.reshape(N_FRONT, F, F) + extra.reshape(N_FRONT, F, F))
    factored = lax.map(factor_front, assembled)
    return factored.reshape(front_entries.shape)
```

```python
import functools
import jax
import jax.numpy as jnp
from jax import lax
from jax.experimental import pallas as pl
from jax.experimental.pallas import tpu as pltpu
from jax.sharding import PartitionSpec as P

BLOCK = 128
LEAD = 1024
LB = LEAD // BLOCK
FRONTS = 8
GRID = 16
SIDE = 4
DEVICES = FRONTS * GRID
FB = 32
TB = FB - LB
TILES = 128
PBINS = FRONTS * TB * LB
TSLOTS = 32
TBINS = DEVICES * TSLOTS
BINS = PBINS + TBINS
SUB = 8
ACCS = 8
UNROLL = 32
VMEM_LIMIT = 60 << 20

highest = lax.Precision.HIGHEST
ANY = pl.BlockSpec(memory_space=pl.ANY)
VMEM = pl.BlockSpec(memory_space=pltpu.VMEM)
SMEM = pl.BlockSpec(memory_space=pltpu.SMEM)


def tdot(a, b):
    return lax.dot_general(
        a, b, (((0,), (0,)), ((), ())), precision=highest, preferred_element_type=jnp.float32
    )


def gather_small(values, axis, size):
    bit = 1
    while bit < size:
        other = lax.ppermute(values, axis, [(i, i ^ bit) for i in range(size)])
        upper = (lax.axis_index(axis) & bit) != 0
        values = jnp.where(
            upper, jnp.concatenate([other, values], 0), jnp.concatenate([values, other], 0)
        )
        bit *= 2
    return values


def ring_perm(along_x, step):
    def to(i):
        x, y = divmod(i, SIDE)
        return ((x + step) % SIDE) * SIDE + y if along_x else x * SIDE + (y + step) % SIDE

    return [(i, to(i)) for i in range(GRID)]


def ring(block, along_x):
    up, down = ring_perm(along_x, 1), ring_perm(along_x, -1)
    half = block.shape[0] // 2
    from_prev = lax.ppermute(block, "grid", up)
    from_next = lax.ppermute(block, "grid", down)
    far_a = lax.ppermute(from_prev[:half], "grid", up)
    far_b = lax.ppermute(from_next[half:], "grid", down)
    return block, from_next, far_a, far_b, from_prev


def gather_rings(rows):
    half = rows.shape[0] // 2
    out = []
    for part, first_x in ((rows[:half], True), (rows[half:], False)):
        own, nxt, far_a, far_b, prv = ring(part, first_x)
        line = jnp.stack([own, nxt, jnp.concatenate([far_a, far_b], 0), prv], 0)
        out.extend(ring(line, not first_x))
    return out


def copy_pieces(pieces, dst, sem, position, start_row, rows):
    x, y = position // SIDE, position % SIDE
    half = rows // 2
    copies = []
    for h in range(2):
        own, nxt, far_a, far_b, prv = pieces[5 * h : 5 * h + 5]
        for outer in range(SIDE):
            for inner in range(SIDE):
                if outer == 2:
                    src = (far_a if inner < 2 else far_b).at[inner % 2]
                else:
                    src = (own, nxt, None, prv)[outer].at[inner]
                dx, dy = (inner, outer) if h == 0 else (outer, inner)
                g = ((x + dx) % SIDE) * SIDE + (y + dy) % SIDE
                copies.append(
                    pltpu.make_async_copy(
                        src,
                        dst.at[
                            pl.ds(start_row + h * half, half),
                            pl.ds(pl.multiple_of(g * SUB, SUB), SUB),
                            :,
                        ],
                        sem.at[h * 16 + outer * 4 + inner],
                    )
                )
    return copies


def combine_kernel(bins, x, panel, trail, *accs):
    for acc in accs:
        acc[...] = jnp.zeros_like(acc)

    def body(b, carry):
        base = pl.multiple_of(b * UNROLL, UNROLL)
        for first in range(0, UNROLL, ACCS):
            at = [bins[base + first + m] for m in range(ACCS)]
            rows = [x[pl.ds(base + first + m, 1), :] for m in range(ACCS)]
            sums = [accs[m][pl.ds(at[m], 1), :] + rows[m] for m in range(ACCS)]
            for m in range(ACCS):
                accs[m][pl.ds(at[m], 1), :] = sums[m]
        return carry

    lax.fori_loop(0, x.shape[0] // UNROLL, body, 0)
    step = 256

    def finish(out, offset):
        def add(b, carry):
            start = pl.multiple_of(b * step, step)
            total = accs[0][pl.ds(offset + start, step), :]
            for acc in accs[1:]:
                total = total + acc[pl.ds(offset + start, step), :]
            out[pl.ds(start, step), :] = total
            return carry

        lax.fori_loop(0, out.shape[0] // step, add, 0)

    finish(panel, 0)
    finish(trail, PBINS)


def combine(bins, rows):
    return pl.pallas_call(
        combine_kernel,
        out_shape=[
            jax.ShapeDtypeStruct((PBINS, BLOCK), jnp.float32),
            jax.ShapeDtypeStruct((TBINS, BLOCK), jnp.float32),
        ],
        in_specs=[SMEM, VMEM],
        out_specs=[VMEM, VMEM],
        scratch_shapes=[pltpu.VMEM((BINS, BLOCK), jnp.float32)] * ACCS,
        compiler_params=pltpu.CompilerParams(vmem_limit_bytes=VMEM_LIMIT),
        name="combine",
    )(bins, rows)


def factor_rows(rows, first, sub):
    for j in range(SUB):
        scale = lax.rsqrt(rows[j : j + 1, first + j : first + j + 1])
        pivot = rows[j : j + 1, :] * scale
        weight = jnp.where(sub > j, rows[:, first + j : first + j + 1] * scale, 0.0)
        rows = jnp.where(sub == j, pivot, rows - weight * pivot)
    return rows


def factor_kernel(position, *refs):
    pieces, (own_rows, inverse, entries, work, diag, pair, sem) = refs[:10], refs[10:]
    copies = copy_pieces(pieces, entries, sem, position[0], 0, LB)
    for copy in copies:
        copy.start()
    for copy in copies:
        copy.wait()
    sub = lax.broadcasted_iota(jnp.int32, (SUB, 1), 0)
    row = lax.broadcasted_iota(jnp.int32, (BLOCK, BLOCK), 0)
    col = lax.broadcasted_iota(jnp.int32, (BLOCK, BLOCK), 1)
    eye = jnp.where(row == col, 1.0, 0.0)
    for r in range(LB):
        for c in range(r + 1):
            block = entries[r, :, c * BLOCK : (c + 1) * BLOCK]
            if r == c:
                block = jnp.where(col <= row, block, 0.0)
                block = block + jnp.where(col < row, block, 0.0).T
                work[r * BLOCK : (r + 1) * BLOCK, r * BLOCK : (r + 1) * BLOCK] = block
            else:
                work[c * BLOCK : (c + 1) * BLOCK, r * BLOCK : (r + 1) * BLOCK] = block.T

    def step(k, carry):
        at = pl.ds(pl.multiple_of(k * BLOCK, BLOCK), BLOCK)
        pair[:, :BLOCK] = work[at, at]
        pair[:, BLOCK:] = eye
        for q in range(BLOCK // SUB):
            first = SUB * q
            rows = pair[first : first + SUB, :]
            if q > 0:
                rows = rows - tdot(pair[0:first, first : first + SUB], pair[0:first, :])
            pair[first : first + SUB, :] = factor_rows(rows, first, sub)
        block_inverse = pair[:, BLOCK:]
        diag[k] = pair[:, :BLOCK]
        work[at, :] = jnp.dot(
            block_inverse, work[at, :], precision=highest, preferred_element_type=jnp.float32
        )
        work[at, at] = block_inverse

        def update(i, inner):
            below = pl.ds(pl.multiple_of(i * BLOCK, BLOCK), BLOCK)
            work[below, at] = jnp.zeros((BLOCK, BLOCK), jnp.float32)
            work[below, :] = work[below, :] - tdot(work[at, below], work[at, :])
            return inner

        lax.fori_loop(k + 1, LB, update, 0)
        return carry

    lax.fori_loop(0, LB, step, 0)
    for k in range(LB):
        at = slice(k * BLOCK, (k + 1) * BLOCK)
        inverse[at, : (k + 1) * BLOCK] = work[at, : (k + 1) * BLOCK]
        if k + 1 < LB:
            inverse[at, (k + 1) * BLOCK :] = jnp.zeros((BLOCK, LEAD - (k + 1) * BLOCK), jnp.float32)
    mine = jnp.minimum(position[0], LB - 1)
    mine_at = pl.ds(pl.multiple_of(mine * BLOCK, BLOCK), BLOCK)
    for k in range(LB):
        at = slice(k * BLOCK, (k + 1) * BLOCK)
        block = jnp.where(k == mine, jnp.where(row <= col, diag[k], 0.0), work[at, mine_at])
        own_rows[:, at] = jnp.where(k <= mine, block, 0.0).T


def factor(position, pieces):
    return pl.pallas_call(
        factor_kernel,
        out_shape=[
            jax.ShapeDtypeStruct((BLOCK, LEAD), jnp.float32),
            jax.ShapeDtypeStruct((LEAD, LEAD), jnp.float32),
        ],
        in_specs=[SMEM] + [ANY] * 10,
        out_specs=[VMEM, VMEM],
        scratch_shapes=[
            pltpu.VMEM((LB, BLOCK, LEAD), jnp.float32),
            pltpu.VMEM((LEAD, LEAD), jnp.float32),
            pltpu.VMEM((LB, BLOCK, BLOCK), jnp.float32),
            pltpu.VMEM((BLOCK, 2 * BLOCK), jnp.float32),
            pltpu.SemaphoreType.DMA((32,)),
        ],
        compiler_params=pltpu.CompilerParams(vmem_limit_bytes=VMEM_LIMIT),
        cost_estimate=pl.CostEstimate(flops=120 * 10**9, bytes_accessed=20 << 20, transcendentals=1024),
        name="factor",
    )(position, *pieces)


def split(values):
    high = values.astype(jnp.bfloat16)
    return high, (values - high.astype(jnp.float32)).astype(jnp.bfloat16)


def update_kernel(position, *refs):
    pieces, (entries, lead_rows, extra, out, solved, high, low, sem) = refs[:10], refs[10:]
    g = position[0]
    copies = copy_pieces(pieces, solved, sem, g, 0, TB)
    for copy in copies:
        copy.start()
    for copy in copies:
        copy.wait()

    def halves(b, carry):
        high[b], low[b] = split(solved[b])
        return carry

    lax.fori_loop(0, TB, halves, 0)
    top = jnp.maximum(g - LB, 0)
    bottom = FB // 2 + g - LB
    own_high = jnp.concatenate([high[top], high[bottom]], 0)
    own_low = jnp.concatenate([low[top], low[bottom]], 0)
    out[0, :, :LEAD] = jnp.where(g < LB, lead_rows[...], solved[top])
    out[1, :, :LEAD] = solved[bottom]
    row = lax.broadcasted_iota(jnp.int32, (BLOCK, BLOCK), 0)
    col = lax.broadcasted_iota(jnp.int32, (BLOCK, BLOCK), 1)

    def mul(a, b):
        return lax.dot_general(a, b, (((1,), (1,)), ((), ())), preferred_element_type=jnp.float32)

    for c in range(0, TB, 2):
        col_high = high[c : c + 2].reshape(2 * BLOCK, LEAD)
        col_low = low[c : c + 2].reshape(2 * BLOCK, LEAD)
        product = mul(own_high, col_high) + (mul(own_high, col_low) + mul(own_low, col_high))
        for n in range(2):
            block = LB + c + n
            at = slice(block * BLOCK, (block + 1) * BLOCK)
            for local in range(2):
                row_block = local * (FB // 2) + g
                slot = c + n if local == 1 else jnp.minimum(LB + 1 + g + c + n, TSLOTS - 1)
                value = entries[local, :, at] + extra[slot]
                value = value - product[
                    local * BLOCK : (local + 1) * BLOCK, n * BLOCK : (n + 1) * BLOCK
                ]
                inside = (block * BLOCK + col) <= (row_block * BLOCK + row)
                out[local, :, at] = jnp.where(inside, value, 0.0)


def update(position, pieces, entries, lead_rows, extra):
    return pl.pallas_call(
        update_kernel,
        out_shape=jax.ShapeDtypeStruct(entries.shape, jnp.float32),
        in_specs=[SMEM] + [ANY] * 10 + [VMEM] * 3,
        out_specs=VMEM,
        scratch_shapes=[
            pltpu.VMEM((TB, BLOCK, LEAD), jnp.float32),
            pltpu.VMEM((TB, BLOCK, LEAD), jnp.bfloat16),
            pltpu.VMEM((TB, BLOCK, LEAD), jnp.bfloat16),
            pltpu.SemaphoreType.DMA((32,)),
        ],
        compiler_params=pltpu.CompilerParams(vmem_limit_bytes=VMEM_LIMIT),
        name="update",
    )(position, *pieces, entries, lead_rows, extra)


def destination_bins(owners, local_rows, picks):
    front, g = owners // GRID, owners % GRID
    shifted = local_rows + (local_rows * GRID + g < LB).astype(jnp.int32)
    row_block = shifted * GRID + g
    col_block = picks % (row_block + 1)
    panel = (front * TB + row_block - LB) * LB + col_block
    slot = col_block - LB + jnp.where(row_block < GRID, LB + 1 + g, 0)
    trail = PBINS + (g * FRONTS + front) * TSLOTS + slot
    return jnp.where(col_block < LB, panel, trail)


def local(front_entries, child_tiles, tile_owner, tile_rows, tile_picks):
    both = ("grid", "front")
    g = lax.axis_index("grid")
    position = g.astype(jnp.int32).reshape(1)
    entries = front_entries[0, :, 0]
    panel = entries[:, :, :LEAD].reshape(2, GRID, SUB, LEAD)
    panel = lax.all_to_all(panel, "grid", split_axis=1, concat_axis=1)
    panel = panel.reshape(FB, SUB, LEAD)
    bins = destination_bins(tile_owner[0, :, 0], tile_rows[0], tile_picks[0])
    bins = gather_small(gather_small(bins[None], "front", FRONTS), "grid", GRID).reshape(-1)
    tile_rows_in = lax.all_to_all(child_tiles[0], both, split_axis=1, concat_axis=0)
    lead_rows, inverse = factor(position, gather_rings(panel[:LB]))
    panel_sums, trail_sums = combine(bins, tile_rows_in.reshape(DEVICES * TILES, BLOCK))
    panel_sums = lax.all_to_all(
        panel_sums.reshape(FRONTS, TB, LB, BLOCK), "front", split_axis=0, concat_axis=0
    )
    panel_sums = panel_sums.transpose(1, 0, 2, 3).reshape(TB, SUB, LEAD)
    below = (panel[LB:] + panel_sums).reshape(TB * SUB, LEAD)
    solved = lax.dot_general(below, inverse, (((1,), (1,)), ((), ())), precision=highest)
    pieces = gather_rings(solved.reshape(TB, SUB, LEAD))
    extra = lax.all_to_all(
        trail_sums.reshape(DEVICES, TSLOTS, BLOCK), both, split_axis=0, concat_axis=0
    )
    out = update(position, pieces, entries, lead_rows, extra.transpose(1, 0, 2))
    return out[None, :, None]


def solution(mesh):
    return jax.shard_map(
        local,
        mesh=mesh,
        in_specs=(
            P("front", None, "grid", None, None),
            P("front", "grid", None, None),
            P("front", "grid", None),
            P("front", "grid"),
            P("front", "grid"),
        ),
        out_specs=P("front", None, "grid", None, None),
        check_vma=False,
    )
```

```python
import functools
import jax
import jax.numpy as jnp
from jax import lax
from jax.experimental import pallas as pl
from jax.experimental.pallas import tpu as pltpu
from jax.sharding import Mesh
from jax.sharding import PartitionSpec as P

BLOCK = 128
LEAD = 1024
LB = LEAD // BLOCK
FRONTS = 8
GRID = 16
SIDE = 4
DEVICES = FRONTS * GRID
FB = 32
TB = FB - LB
TILES = 128
LINES = TB // SIDE
SLICE = BLOCK // SIDE
PSLOTS = LINES * LB
TSLOTS = 88
SLOTS = PSLOTS + TSLOTS
BINS = SIDE * FRONTS * SLOTS
OUT_SLOTS = 2 + LINES
SUB = 8
SLABS = BLOCK // SUB
ACCS = 8
VMEM_LIMIT = 60 << 20

highest = lax.Precision.HIGHEST
ANY = pl.BlockSpec(memory_space=pl.ANY)
VMEM = pl.BlockSpec(memory_space=pltpu.VMEM)
SMEM = pl.BlockSpec(memory_space=pltpu.SMEM)


def split(values):
    high = values.astype(jnp.bfloat16)
    return high, (values - high.astype(jnp.float32)).astype(jnp.bfloat16)


def mul(a, b):
    return lax.dot_general(a, b, (((1,), (1,)), ((), ())), preferred_element_type=jnp.float32)


def tdot(a, b):
    return lax.dot_general(
        a, b, (((0,), (0,)), ((), ())), precision=highest, preferred_element_type=jnp.float32
    )


def shift(block, axis, step):
    return lax.ppermute(block, axis, [(i, (i + step) % SIDE) for i in range(SIDE)])


def ring(block, axis):
    half = block.shape[0] // 2
    from_prev = shift(block, axis, 1)
    from_next = shift(block, axis, -1)
    far_a = shift(from_prev[:half], axis, 1)
    far_b = shift(from_next[half:], axis, -1)
    return block, from_next, far_a, far_b, from_prev


def ring_copies(pieces, here, place, sem, first_sem):
    own, nxt, far_a, far_b, prv = pieces
    parts = [(own, 0, None), (nxt, 1, None), (far_a, 2, 0), (far_b, 2, 1), (prv, 3, None)]
    return [
        pltpu.make_async_copy(src, place((here + step) % SIDE, part), sem.at[first_sem + n])
        for n, (src, step, part) in enumerate(parts)
    ]


def gather_lines(first, second, tied):
    lines = []
    for part, axis in ((first, "x"), (second, "y")):
        lines.append(jnp.stack([part, *(shift(part, axis, -n) for n in range(1, SIDE))]))
    *lines, tied = lax.optimization_barrier((*lines, tied))
    return [*ring(lines[0], "y"), *ring(lines[1], "x")], tied


def line_copies(pieces, place, sem, x, y):
    copies = []
    for h in range(2):
        own, nxt, far_a, far_b, prv = pieces[5 * h : 5 * h + 5]
        for outer in range(SIDE):
            for inner in range(SIDE):
                if outer == 2:
                    src = (far_a if inner < 2 else far_b).at[inner % 2]
                else:
                    src = (own, nxt, None, prv)[outer].at[inner]
                dx, dy = (inner, outer) if h == 0 else (outer, inner)
                dst = place(h, (x + dx) % SIDE, (y + dy) % SIDE)
                copies.append(pltpu.make_async_copy(src, dst, sem.at[len(copies)]))
    return copies


def combine_kernel(bins, x, out, *accs):
    sources = x.shape[0] // TILES

    @pl.when(pl.program_id(0) == 0)
    def _():
        for acc in accs:
            acc[...] = jnp.zeros_like(acc)

    group = 32

    def body(q, carry):
        base = pl.multiple_of(q * group, group)
        labels = pl.program_id(0) * (sources * TILES) + base
        for first in range(0, group, ACCS):
            at = [bins[labels + first + m] for m in range(ACCS)]
            rows = [x[pl.ds(base + first + m, 1), :] for m in range(ACCS)]
            sums = [accs[m][pl.ds(at[m], 1), :] + rows[m] for m in range(ACCS)]
            for m in range(ACCS):
                accs[m][pl.ds(at[m], 1), :] = sums[m]
        return carry

    lax.fori_loop(0, x.shape[0] // group, body, 0)
    step = 256

    @pl.when(pl.program_id(0) == pl.num_programs(0) - 1)
    def _():
        def add(b, carry):
            at = pl.ds(pl.multiple_of(b * step, step), step)
            total = accs[0][at, :]
            for acc in accs[1:]:
                total = total + acc[at, :]
            out[at, :] = total
            return carry

        lax.fori_loop(0, BINS // step, add, 0)


def combine(bins, rows):
    steps = 4
    return pl.pallas_call(
        combine_kernel,
        grid=(steps,),
        out_shape=jax.ShapeDtypeStruct((BINS, BLOCK), jnp.float32),
        in_specs=[SMEM, pl.BlockSpec((rows.shape[0] // steps, BLOCK), lambda i: (i, 0))],
        out_specs=pl.BlockSpec((BINS, BLOCK), lambda i: (0, 0)),
        scratch_shapes=[pltpu.VMEM((BINS, BLOCK), jnp.float32)] * ACCS,
        compiler_params=pltpu.CompilerParams(vmem_limit_bytes=VMEM_LIMIT),
        cost_estimate=pl.CostEstimate(flops=20 * 10**9, bytes_accessed=20 << 20, transcendentals=0),
        name="combine",
    )(bins, rows)


def factor_rows(rows, first, sub):
    def spread(values, j):
        return jnp.broadcast_to(values[j : j + 1, :], values.shape)

    columns = [
        jnp.broadcast_to(rows[:, first + j : first + j + 1], (SUB, BLOCK)) for j in range(SUB)
    ]
    parts = [rows[:, :BLOCK], rows[:, BLOCK:]]
    for j in range(SUB):
        scale = lax.rsqrt(spread(columns[j], j))
        weight = jnp.where(sub > j, columns[j] * scale, 0.0)
        for m in range(j + 1, SUB):
            columns[m] = columns[m] - weight * (spread(columns[m], j) * scale)
        for n in range(2):
            pivot = spread(parts[n], j) * scale
            parts[n] = jnp.where(sub == j, pivot, parts[n] - weight * pivot)
    return jnp.concatenate(parts, 1)


def factor_kernel(position, *refs):
    pieces, (own_rows, inverse_high, inverse_low, entries, work, diag, pair, sem) = refs[:10], refs[10:]
    px, py = position[0], position[1]

    def place(h, x, y):
        block = (x % 2) * SIDE + y
        slab = block * SLABS + (x // 2) * (SLABS // 2) + h * (SLABS // 4)
        return entries.at[pl.ds(slab, SLABS // 4)]

    copies = line_copies(pieces, place, sem, px, py)
    for copy in copies:
        copy.start()
    for copy in copies:
        copy.wait()
    sub = lax.broadcasted_iota(jnp.int32, (SUB, 1), 0)
    row = lax.broadcasted_iota(jnp.int32, (BLOCK, BLOCK), 0)
    col = lax.broadcasted_iota(jnp.int32, (BLOCK, BLOCK), 1)
    eye = jnp.where(row == col, 1.0, 0.0)
    for r in range(LB):
        for c in range(r + 1):
            block = entries[r * SLABS : (r + 1) * SLABS, :, c * BLOCK : (c + 1) * BLOCK]
            block = block.reshape(BLOCK, BLOCK)
            if r == c:
                block = jnp.where(col <= row, block, 0.0)
                block = block + jnp.where(col < row, block, 0.0).T
                work[r * BLOCK : (r + 1) * BLOCK, r * BLOCK : (r + 1) * BLOCK] = block
            else:
                work[c * BLOCK : (c + 1) * BLOCK, r * BLOCK : (r + 1) * BLOCK] = block.T

    def step(k, carry):
        at = pl.ds(pl.multiple_of(k * BLOCK, BLOCK), BLOCK)
        pair[:, :BLOCK] = work[at, at]
        pair[:, BLOCK:] = eye
        for q in range(BLOCK // SUB):
            first = SUB * q
            rows = pair[first : first + SUB, :]
            if q > 0:
                rows = rows - tdot(pair[0:first, first : first + SUB], pair[0:first, :])
            pair[first : first + SUB, :] = factor_rows(rows, first, sub)
        block_inverse = pair[:, BLOCK:]
        diag[k] = pair[:, :BLOCK]
        work[at, :] = jnp.dot(
            block_inverse, work[at, :], precision=highest, preferred_element_type=jnp.float32
        )
        work[at, at] = block_inverse

        def update(i, inner):
            below = pl.ds(pl.multiple_of(i * BLOCK, BLOCK), BLOCK)
            work[below, at] = jnp.zeros((BLOCK, BLOCK), jnp.float32)
            work[below, :] = work[below, :] - tdot(work[at, below], work[at, :])
            return inner

        lax.fori_loop(k + 1, LB, update, 0)
        return carry

    lax.fori_loop(0, LB, step, 0)
    for k in range(LB):
        at = slice(k * BLOCK, (k + 1) * BLOCK)
        done = slice(0, (k + 1) * BLOCK)
        inverse_high[at, done], inverse_low[at, done] = split(work[at, done])
        if k + 1 < LB:
            rest = jnp.zeros((BLOCK, LEAD - (k + 1) * BLOCK), jnp.bfloat16)
            inverse_high[at, (k + 1) * BLOCK :] = rest
            inverse_low[at, (k + 1) * BLOCK :] = rest
    mine = jnp.minimum(px * SIDE + py, LB - 1)
    mine_at = pl.ds(pl.multiple_of(mine * BLOCK, BLOCK), BLOCK)
    for k in range(LB):
        at = slice(k * BLOCK, (k + 1) * BLOCK)
        block = jnp.where(k == mine, jnp.where(row <= col, diag[k], 0.0), work[at, mine_at])
        own_rows[:, at] = jnp.where(k <= mine, block, 0.0).T


def factor(position, pieces):
    return pl.pallas_call(
        factor_kernel,
        out_shape=[
            jax.ShapeDtypeStruct((BLOCK, LEAD), jnp.float32),
            jax.ShapeDtypeStruct((LEAD, LEAD), jnp.bfloat16),
            jax.ShapeDtypeStruct((LEAD, LEAD), jnp.bfloat16),
        ],
        in_specs=[SMEM] + [ANY] * 10,
        out_specs=[VMEM] * 3,
        scratch_shapes=[
            pltpu.VMEM((LB * SLABS, SUB, LEAD), jnp.float32),
            pltpu.VMEM((LEAD, LEAD), jnp.float32),
            pltpu.VMEM((LB, BLOCK, BLOCK), jnp.float32),
            pltpu.VMEM((BLOCK, 2 * BLOCK), jnp.float32),
            pltpu.SemaphoreType.DMA((32,)),
        ],
        compiler_params=pltpu.CompilerParams(vmem_limit_bytes=VMEM_LIMIT),
        cost_estimate=pl.CostEstimate(flops=120 * 10**9, bytes_accessed=20 << 20, transcendentals=1024),
        name="factor",
    )(position, *pieces)


def solve_kernel(position, own, part1, part2, part3, sums, inverse_high, inverse_low, out, rows):
    x = position[0]
    for step, part in enumerate((own, part1, part2, part3)):
        source = (x + SIDE - step) % SIDE
        for l in range(2):
            rows[SIDE * l + source] = part[l]
    for m in range(LINES):
        for c in range(LB):
            at = slice(c * BLOCK, (c + 1) * BLOCK)
            values = sums[pl.ds(m * LB + c, SLICE, stride=SLOTS), :]
            rows[LB // SIDE + m, :, at] = rows[LB // SIDE + m, :, at] + values
    high, low = split(rows[LB // SIDE :].reshape(LINES * SLICE, LEAD))
    wide = 2 * BLOCK
    for c in range(LEAD // wide):
        end = (c + 1) * wide
        inv_high = inverse_high[end - wide : end, :end]
        inv_low = inverse_low[end - wide : end, :end]
        value = mul(high[:, :end], inv_high) + (
            mul(high[:, :end], inv_low) + mul(low[:, :end], inv_high)
        )
        out[:, :, end - wide : end] = value.reshape(LINES, SLICE, wide)


def solve(position, parts, sums, inverse_high, inverse_low):
    return pl.pallas_call(
        solve_kernel,
        out_shape=jax.ShapeDtypeStruct((LINES, SLICE, LEAD), jnp.float32),
        in_specs=[SMEM] + [VMEM] * 7,
        out_specs=VMEM,
        scratch_shapes=[pltpu.VMEM((2 * SIDE, SLICE, LEAD), jnp.float32)],
        compiler_params=pltpu.CompilerParams(vmem_limit_bytes=VMEM_LIMIT),
        name="solve",
    )(position, *parts, sums, inverse_high, inverse_low)


def product_kernel(position, *refs):
    along_x, along_y, (sums, out, own, cols, rows, high, low, sem) = refs[:5], refs[5:10], refs[10:]
    x, y = position[0], position[1]
    half = LINES // 2

    def place_cols(index, part):
        at = pl.ds(pl.multiple_of(index * SLICE, SLICE), SLICE)
        span = pl.ds(0, LINES) if part is None else pl.ds(part * half, half)
        return cols.at[span, at, :]

    def place_rows(index, part):
        start, count = (0, LINES) if part is None else (part * half, half)
        return rows.at[index, pl.ds(start, count)]

    copies = ring_copies(along_x, x, place_cols, sem, 0)
    copies += ring_copies(along_y, y, place_rows, sem, 5)
    for copy in copies:
        copy.start()
    for copy in copies[:5]:
        copy.wait()
    for m in range(LINES):
        at = slice(m * BLOCK, (m + 1) * BLOCK)
        high[at], low[at] = split(cols[m])
    own[0] = cols[jnp.maximum(x - 2, 0)]
    own[1] = cols[x + 2]
    for copy in copies[5:]:
        copy.wait()
    for z in range(SIDE):
        row_high, row_low = split(rows[z].reshape(LINES * SLICE, LEAD))
        value = mul(row_high, high[...]) + (mul(row_high, low[...]) + mul(row_low, high[...]))
        for m in range(LINES):
            row_block = LB + z + SIDE * m
            owner, first = row_block % GRID, 2 if row_block >= GRID else 0
            for n in range(LINES if first else 2):
                below = jnp.maximum(row_block - LB - y - SIDE * n, 0)
                slot = (TB - y) * n - 2 * n * (n - 1) + below
                out[owner, first + n] = sums[pl.ds(PSLOTS + slot, SLICE, stride=SLOTS), :] - value[
                    m * SLICE : (m + 1) * SLICE, n * BLOCK : (n + 1) * BLOCK
                ]
    for owner in range(LB):
        for n in range(2):
            out[owner, n] = jnp.zeros((SLICE, BLOCK), jnp.float32)


def product(position, along_x, along_y, sums):
    return pl.pallas_call(
        product_kernel,
        out_shape=[
            jax.ShapeDtypeStruct((GRID, OUT_SLOTS, SLICE, BLOCK), jnp.float32),
            jax.ShapeDtypeStruct((2, BLOCK, LEAD), jnp.float32),
        ],
        in_specs=[SMEM] + [ANY] * 10 + [VMEM],
        out_specs=[VMEM] * 2,
        scratch_shapes=[
            pltpu.VMEM((LINES, BLOCK, LEAD), jnp.float32),
            pltpu.VMEM((SIDE, LINES, SLICE, LEAD), jnp.float32),
            pltpu.VMEM((LINES * BLOCK, LEAD), jnp.bfloat16),
            pltpu.VMEM((LINES * BLOCK, LEAD), jnp.bfloat16),
            pltpu.SemaphoreType.DMA((10,)),
        ],
        compiler_params=pltpu.CompilerParams(vmem_limit_bytes=VMEM_LIMIT),
        name="product",
    )(position, *along_x, *along_y, sums)


def finish_kernel(position, entries, lead_rows, own, change, out):
    g = position[0] * SIDE + position[1]
    row = lax.broadcasted_iota(jnp.int32, (SLICE, BLOCK), 0)
    col = lax.broadcasted_iota(jnp.int32, (SLICE, BLOCK), 1)
    out[0, :, :LEAD] = jnp.where(g < LB, lead_rows[...], own[0])
    out[1, :, :LEAD] = own[1]
    for local in range(2):
        row_block = local * GRID + g
        for block in range(LB, FB):
            at = slice(block * BLOCK, (block + 1) * BLOCK)
            y, n = block % SIDE, (block - LB) // SIDE
            if local == 0 and n >= 2:
                out[local, :, at] = jnp.zeros((BLOCK, BLOCK), jnp.float32)
                continue
            for x in range(SIDE):
                span = slice(x * SLICE, (x + 1) * SLICE)
                value = entries[local, span, at] + change[x * SIDE + y, 2 * local + n]
                inside = (block * BLOCK + col) <= (row_block * BLOCK + x * SLICE + row)
                out[local, span, at] = jnp.where(inside, value, 0.0)


def finish(position, entries, lead_rows, own, change):
    return pl.pallas_call(
        finish_kernel,
        out_shape=jax.ShapeDtypeStruct(entries.shape, jnp.float32),
        in_specs=[SMEM] + [VMEM] * 4,
        out_specs=VMEM,
        compiler_params=pltpu.CompilerParams(vmem_limit_bytes=VMEM_LIMIT),
        name="finish",
    )(position, entries, lead_rows, own, change)


def destination_bins(owners, local_rows, picks):
    front, g = owners // GRID, owners % GRID
    shifted = local_rows + (local_rows * GRID + g < LB).astype(jnp.int32)
    row_block = shifted * GRID + g
    col_block = picks % (row_block + 1)
    panel = (row_block % SIDE * FRONTS + front) * SLOTS + (row_block - LB) // SIDE * LB + col_block
    y, n = col_block % SIDE, (col_block - LB) // SIDE
    slot = (TB - y) * n - 2 * n * (n - 1) + row_block - col_block
    trail = (y * FRONTS + front) * SLOTS + PSLOTS + slot
    return jnp.where(col_block < LB, panel, trail)


def across(values, axes):
    return lax.all_to_all(values, axes, split_axis=0, concat_axis=0)


def local(front_entries, child_tiles, tile_owner, tile_rows, tile_picks):
    x, y = lax.axis_index("x"), lax.axis_index("y")
    position = jnp.stack([x, y]).astype(jnp.int32)
    entries = front_entries[0, :, 0]
    half = BLOCK // 2
    lead = entries[0, :, :LEAD]
    other = lax.ppermute(lead[half:], "x", [(0, 2), (1, 3)])
    lead = jnp.where(x < 2, lead[:half], other).reshape(SLABS // 2, SUB, LEAD)
    bins = destination_bins(tile_owner[0, :, 0], tile_rows[0], tile_picks[0])
    bins = across(jnp.broadcast_to(bins, (DEVICES, 1, TILES)), ("x", "y", "front")).reshape(-1)
    lead, bins, tiles = lax.optimization_barrier((lead, bins, child_tiles))
    half = SLABS // 4
    lead, tiles = gather_lines(lead[:half], lead[half:], tiles[0].transpose(1, 0, 2))
    tiles, lead, entries = lax.optimization_barrier((tiles, lead, entries))
    rows = across(tiles, ("x", "y", "front")).reshape(-1, BLOCK)
    panel = entries[:, :, :LEAD].reshape(2, SIDE, SLICE, LEAD)
    panel = [
        lax.dynamic_index_in_dim(panel, (x + n) % SIDE, 1, keepdims=False) for n in range(SIDE)
    ]
    panel = [part if n == 0 else shift(part, "x", n) for n, part in enumerate(panel)]
    lead_rows, *inverse = factor(position, lead)
    bins, lead_rows, panel = lax.optimization_barrier((bins, lead_rows, panel))
    sums = combine(bins, rows).reshape(SLICE, SLOTS, BLOCK)
    sums = across(sums, ("y", "front")).reshape(-1, BLOCK)
    solved = solve(position, panel, sums, *inverse)
    change, own = product(position, ring(solved, "x"), ring(solved, "y"), sums)
    change = across(change, ("x", "y"))
    out = finish(position, entries, lead_rows, own, change)
    return out[None, :, None]


def solution(mesh):
    mesh = Mesh(mesh.devices.reshape(FRONTS, SIDE, SIDE), ("front", "x", "y"))
    grid = ("x", "y")
    return jax.shard_map(
        local,
        mesh=mesh,
        in_specs=(
            P("front", None, grid, None, None),
            P("front", grid, None, None),
            P("front", grid, None),
            P("front", grid),
            P("front", grid),
        ),
        out_specs=P("front", None, grid, None, None),
        check_vma=False,
    )
```

```python
import functools
import jax
import jax.numpy as jnp
from jax import lax
from jax.experimental import pallas as pl
from jax.experimental.pallas import tpu as pltpu
from jax.sharding import Mesh
from jax.sharding import PartitionSpec as P

BLOCK = 128
LEAD = 1024
LB = LEAD // BLOCK
FRONTS = 8
GRID = 16
SIDE = 4
DEVICES = FRONTS * GRID
FB = 32
TB = FB - LB
TILES = 128
LINES = TB // SIDE
SLICE = BLOCK // SIDE
PSLOTS = LINES * LB
TSLOTS = 88
PBINS = SIDE * FRONTS * PSLOTS
TBINS = SIDE * FRONTS * TSLOTS
BINS = PBINS + TBINS
OUT_SLOTS = 2 + LINES
SUB = 8
SLABS = BLOCK // SUB
ACCS = 8
VMEM_LIMIT = 60 << 20

highest = lax.Precision.HIGHEST
ANY = pl.BlockSpec(memory_space=pl.ANY)
VMEM = pl.BlockSpec(memory_space=pltpu.VMEM)
SMEM = pl.BlockSpec(memory_space=pltpu.SMEM)


def split(values):
    high = values.astype(jnp.bfloat16)
    return high, (values - high.astype(jnp.float32)).astype(jnp.bfloat16)


def mul(a, b):
    return lax.dot_general(a, b, (((1,), (1,)), ((), ())), preferred_element_type=jnp.float32)


def tdot(a, b):
    return lax.dot_general(
        a, b, (((0,), (0,)), ((), ())), precision=highest, preferred_element_type=jnp.float32
    )


def shift(block, axis, step):
    return lax.ppermute(block, axis, [(i, (i + step) % SIDE) for i in range(SIDE)])


def gather_front(values):
    others = [
        lax.ppermute(values, "front", [(i, i ^ k) for i in range(FRONTS)]) for k in range(1, FRONTS)
    ]
    return jnp.stack([values, *others])


def ring_near(block, axis):
    return shift(block, axis, -1), shift(block, axis, 1)


def ring_far(near, axis):
    from_next, from_prev = near
    half = from_prev.shape[0] // 2
    return shift(from_prev[:half], axis, 1), shift(from_next[half:], axis, -1)


def ring_pieces(block, near, far):
    return [block, near[0], *far, near[1]]


def gather_lines(first, second, given, work):
    lines = []
    for part, axis in ((first, "x"), (second, "y")):
        lines.append(jnp.stack([part, *(shift(part, axis, -n) for n in range(1, SIDE))]))
    lines, given = lax.optimization_barrier((lines, given))
    near = [ring_near(line, axis) for line, axis in zip(lines, ("y", "x"))]
    near, done = lax.optimization_barrier((near, work(given)))
    far = [ring_far(pair, axis) for pair, axis in zip(near, ("y", "x"))]
    return lines, near, far, done


def line_copies(pieces, place, sem, x, y):
    copies = []
    for h in range(2):
        own, nxt, far_a, far_b, prv = pieces[5 * h : 5 * h + 5]
        for outer in range(SIDE):
            for inner in range(SIDE):
                if outer == 2:
                    src = (far_a if inner < 2 else far_b).at[inner % 2]
                else:
                    src = (own, nxt, None, prv)[outer].at[inner]
                dx, dy = (inner, outer) if h == 0 else (outer, inner)
                for start, count, dst in place(h, (x + dx) % SIDE, (y + dy) % SIDE):
                    copies.append(
                        pltpu.make_async_copy(src.at[pl.ds(start, count)], dst, sem.at[len(copies)])
                    )
    return copies


def turn_kernel(x, out):
    tiles = out.shape[1]

    def body(i, carry):
        for first in range(0, tiles, SUB):
            rows = x[pl.ds(first * BLOCK + i, SUB, stride=BLOCK), :]
            out[i, first : first + SUB, :] = rows
        return carry

    lax.fori_loop(0, BLOCK, body, 0, unroll=4)


def turn(tiles):
    step = 64
    return pl.pallas_call(
        turn_kernel,
        grid=(TILES // step,),
        out_shape=jax.ShapeDtypeStruct((BLOCK, TILES, BLOCK), jnp.float32),
        in_specs=[pl.BlockSpec((step * BLOCK, BLOCK), lambda n: (n, 0))],
        out_specs=pl.BlockSpec((BLOCK, step, BLOCK), lambda n: (0, n, 0)),
        compiler_params=pltpu.CompilerParams(vmem_limit_bytes=VMEM_LIMIT),
        cost_estimate=pl.CostEstimate(flops=0, bytes_accessed=16 << 20, transcendentals=0),
        name="turn",
    )(tiles.reshape(TILES * BLOCK, BLOCK))


def combine_kernel(position, bins, x, panel, trail, *accs):
    sources = x.shape[0] // TILES

    @pl.when(pl.program_id(0) == 0)
    def _():
        for acc in accs:
            acc[...] = jnp.zeros_like(acc)

    def body(q, carry):
        source = (q // FRONTS) * FRONTS + jnp.bitwise_xor(q % FRONTS, position[2])
        base = pl.multiple_of(source * TILES, TILES)
        labels = (pl.program_id(0) * sources + q) * TILES
        for first in range(0, TILES, ACCS):
            at = [bins[labels + first + m] for m in range(ACCS)]
            rows = [x[pl.ds(base + first + m, 1), :] for m in range(ACCS)]
            sums = [accs[m][pl.ds(at[m], 1), :] + rows[m] for m in range(ACCS)]
            for m in range(ACCS):
                accs[m][pl.ds(at[m], 1), :] = sums[m]
        return carry

    lax.fori_loop(0, sources, body, 0)
    step = 256

    @pl.when(pl.program_id(0) == pl.num_programs(0) - 1)
    def _():
        for out, offset in ((panel, 0), (trail, PBINS)):

            def add(b, carry, out=out, offset=offset):
                first = pl.multiple_of(b * step, step)
                total = accs[0][pl.ds(offset + first, step), :]
                for acc in accs[1:]:
                    total = total + acc[pl.ds(offset + first, step), :]
                out[pl.ds(first, step), :] = total
                return carry

            lax.fori_loop(0, out.shape[0] // step, add, 0)


def combine(position, bins, rows):
    steps = 4
    sizes = [PBINS, TBINS]
    return pl.pallas_call(
        combine_kernel,
        grid=(steps,),
        out_shape=[jax.ShapeDtypeStruct((size, BLOCK), jnp.float32) for size in sizes],
        in_specs=[SMEM, SMEM, pl.BlockSpec((rows.shape[0] // steps, BLOCK), lambda i: (i, 0))],
        out_specs=[pl.BlockSpec((size, BLOCK), lambda i: (0, 0)) for size in sizes],
        scratch_shapes=[pltpu.VMEM((BINS, BLOCK), jnp.float32)] * ACCS,
        compiler_params=pltpu.CompilerParams(vmem_limit_bytes=VMEM_LIMIT),
        cost_estimate=pl.CostEstimate(flops=20 * 10**9, bytes_accessed=20 << 20, transcendentals=0),
        name="combine",
    )(position, bins, rows)


def factor_rows(rows, first, sub):
    def spread(values, j):
        return jnp.broadcast_to(values[j : j + 1, :], values.shape)

    columns = [
        jnp.broadcast_to(rows[:, first + j : first + j + 1], (SUB, BLOCK)) for j in range(SUB)
    ]
    parts = [rows[:, :BLOCK], rows[:, BLOCK:]]
    for j in range(SUB):
        scale = lax.rsqrt(spread(columns[j], j))
        weight = jnp.where(sub > j, columns[j] * scale, 0.0)
        for m in range(j + 1, SUB):
            columns[m] = columns[m] - weight * (spread(columns[m], j) * scale)
        for n in range(2):
            pivot = spread(parts[n], j) * scale
            parts[n] = jnp.where(sub == j, pivot, parts[n] - weight * pivot)
    return jnp.concatenate(parts, 1)


def factor_kernel(position, *refs):
    pieces, outs, scratch = refs[:10], refs[10:14], refs[14:]
    own_rows, inverse_high, inverse_low, labels = outs
    (entries, labels_in, work, diag, pair, sem) = scratch
    px, py = position[0], position[1]

    def place(h, x, y):
        block = (x % 2) * SIDE + y
        slab = block * SLABS + (x // 2) * (SLABS // 2) + h * (SLABS // 4)
        spans = [(0, SLABS // 4, entries.at[pl.ds(slab, SLABS // 4)])]
        if h == 0:
            spans.append((SLABS // 4, 1, labels_in.at[pl.ds(x * SIDE + y, 1)]))
        return spans

    copies = line_copies(pieces, place, sem, px, py)
    for copy in copies:
        copy.start()
    for copy in copies:
        copy.wait()
    for g in range(GRID):
        labels[g : g + 1, :] = labels_in[g, 0:1, :].astype(jnp.int32)
    sub = lax.broadcasted_iota(jnp.int32, (SUB, 1), 0)
    row = lax.broadcasted_iota(jnp.int32, (BLOCK, BLOCK), 0)
    col = lax.broadcasted_iota(jnp.int32, (BLOCK, BLOCK), 1)
    eye = jnp.where(row == col, 1.0, 0.0)
    for r in range(LB):
        for c in range(r + 1):
            block = entries[r * SLABS : (r + 1) * SLABS, :, c * BLOCK : (c + 1) * BLOCK]
            block = block.reshape(BLOCK, BLOCK)
            if r == c:
                block = jnp.where(col <= row, block, 0.0)
                block = block + jnp.where(col < row, block, 0.0).T
                work[r * BLOCK : (r + 1) * BLOCK, r * BLOCK : (r + 1) * BLOCK] = block
            else:
                work[c * BLOCK : (c + 1) * BLOCK, r * BLOCK : (r + 1) * BLOCK] = block.T

    def step(k, carry):
        at = pl.ds(pl.multiple_of(k * BLOCK, BLOCK), BLOCK)
        pair[:, :BLOCK] = work[at, at]
        pair[:, BLOCK:] = eye
        for q in range(BLOCK // SUB):
            first = SUB * q
            rows = pair[first : first + SUB, :]
            if q > 0:
                rows = rows - tdot(pair[0:first, first : first + SUB], pair[0:first, :])
            pair[first : first + SUB, :] = factor_rows(rows, first, sub)
        block_inverse = pair[:, BLOCK:]
        diag[k] = pair[:, :BLOCK]
        work[at, :] = jnp.dot(
            block_inverse, work[at, :], precision=highest, preferred_element_type=jnp.float32
        )
        work[at, at] = block_inverse

        def update(i, inner):
            below = pl.ds(pl.multiple_of(i * BLOCK, BLOCK), BLOCK)
            work[below, at] = jnp.zeros((BLOCK, BLOCK), jnp.float32)
            work[below, :] = work[below, :] - tdot(work[at, below], work[at, :])
            return inner

        lax.fori_loop(k + 1, LB, update, 0)
        return carry

    lax.fori_loop(0, LB, step, 0)
    for k in range(LB):
        at = slice(k * BLOCK, (k + 1) * BLOCK)
        done = slice(0, (k + 1) * BLOCK)
        inverse_high[at, done], inverse_low[at, done] = split(work[at, done])
        if k + 1 < LB:
            rest = jnp.zeros((BLOCK, LEAD - (k + 1) * BLOCK), jnp.bfloat16)
            inverse_high[at, (k + 1) * BLOCK :] = rest
            inverse_low[at, (k + 1) * BLOCK :] = rest
    mine = jnp.minimum(px * SIDE + py, LB - 1)
    mine_at = pl.ds(pl.multiple_of(mine * BLOCK, BLOCK), BLOCK)
    for k in range(LB):
        at = slice(k * BLOCK, (k + 1) * BLOCK)
        block = jnp.where(k == mine, jnp.where(row <= col, diag[k], 0.0), work[at, mine_at])
        own_rows[:, at] = jnp.where(k <= mine, block, 0.0).T


def factor(position, pieces):
    return pl.pallas_call(
        factor_kernel,
        out_shape=[
            jax.ShapeDtypeStruct((BLOCK, LEAD), jnp.float32),
            jax.ShapeDtypeStruct((LEAD, LEAD), jnp.bfloat16),
            jax.ShapeDtypeStruct((LEAD, LEAD), jnp.bfloat16),
            jax.ShapeDtypeStruct((GRID, LEAD), jnp.int32),
        ],
        in_specs=[SMEM] + [ANY] * 10,
        out_specs=[VMEM] * 4,
        scratch_shapes=[
            pltpu.VMEM((LB * SLABS, SUB, LEAD), jnp.float32),
            pltpu.VMEM((GRID, SUB, LEAD), jnp.float32),
            pltpu.VMEM((LEAD, LEAD), jnp.float32),
            pltpu.VMEM((LB, BLOCK, BLOCK), jnp.float32),
            pltpu.VMEM((BLOCK, 2 * BLOCK), jnp.float32),
            pltpu.SemaphoreType.DMA((48,)),
        ],
        compiler_params=pltpu.CompilerParams(vmem_limit_bytes=VMEM_LIMIT),
        cost_estimate=pl.CostEstimate(flops=120 * 10**9, bytes_accessed=20 << 20, transcendentals=1024),
        name="factor",
    )(position, *pieces)


def solve_kernel(position, own, part1, part2, part3, sums, inverse_high, inverse_low, out, rows):
    x = position[0]
    for step, part in enumerate((own, part1, part2, part3)):
        source = (x + SIDE - step) % SIDE
        for l in range(2):
            rows[SIDE * l + source] = part[l]
    for m in range(LINES):
        for c in range(LB):
            at = slice(c * BLOCK, (c + 1) * BLOCK)
            values = sums[pl.ds(m * LB + c, SLICE, stride=PSLOTS), :]
            rows[LB // SIDE + m, :, at] = rows[LB // SIDE + m, :, at] + values
    high, low = split(rows[LB // SIDE :].reshape(LINES * SLICE, LEAD))
    wide = 2 * BLOCK
    for c in range(LEAD // wide):
        end = (c + 1) * wide
        inv_high = inverse_high[end - wide : end, :end]
        inv_low = inverse_low[end - wide : end, :end]
        value = mul(high[:, :end], inv_high) + (
            mul(high[:, :end], inv_low) + mul(low[:, :end], inv_high)
        )
        out[:, :, end - wide : end] = value.reshape(LINES, SLICE, wide)


def solve(position, parts, sums, inverse_high, inverse_low):
    return pl.pallas_call(
        solve_kernel,
        out_shape=jax.ShapeDtypeStruct((LINES, SLICE, LEAD), jnp.float32),
        in_specs=[SMEM] + [VMEM] * 7,
        out_specs=VMEM,
        scratch_shapes=[pltpu.VMEM((2 * SIDE, SLICE, LEAD), jnp.float32)],
        compiler_params=pltpu.CompilerParams(vmem_limit_bytes=VMEM_LIMIT),
        name="solve",
    )(position, *parts, sums, inverse_high, inverse_low)


def product_kernel(position, *refs):
    along_x, along_y, scratch = refs[:5], refs[5:10], refs[10:]
    sums, out, own, high, low, row_high, row_low = scratch
    x, y = position[0], position[1]
    half = LINES // 2
    out[...] = jnp.zeros_like(out)

    def blocks(pieces, here):
        nearby, nxt, far_a, far_b, prv = pieces
        for step, piece, first in (
            (0, nearby, 0),
            (1, nxt, 0),
            (2, far_a, 0),
            (2, far_b, half),
            (3, prv, 0),
        ):
            for m in range(piece.shape[0]):
                yield (here + step) % SIDE, first + m, piece[m]

    for index, m, values in blocks(along_x, x):
        at = pl.ds(pl.multiple_of(m * BLOCK + index * SLICE, SLICE), SLICE)
        high[at, :], low[at, :] = split(values)
    for l in range(2):
        m = jnp.maximum(x - 2, 0) if l == 0 else x + 2
        nearby, nxt, far_a, far_b, prv = along_x
        for step in range(SIDE):
            at = pl.ds(pl.multiple_of((x + step) % SIDE * SLICE, SLICE), SLICE)
            if step == 2:
                first = far_a[jnp.minimum(m, half - 1)]
                second = far_b[jnp.maximum(m - half, 0)]
                own[l, at, :] = jnp.where(m < half, first, second)
            else:
                own[l, at, :] = (nearby, nxt, None, prv)[step][m]
    for z, m, values in blocks(along_y, y):
        at = pl.ds(pl.multiple_of(m * BLOCK + z * SLICE, SLICE), SLICE)
        row_high[at, :], row_low[at, :] = split(values)
    for pair in range(LINES // 2):
        start = pair * 2 * BLOCK
        rows_high, rows_low = row_high[start:], row_low[start:]
        cols_high, cols_low = high[start : start + 2 * BLOCK], low[start : start + 2 * BLOCK]
        value = mul(rows_high, cols_high) + (mul(rows_high, cols_low) + mul(rows_low, cols_high))
        for row_block in range(LB + 2 * pair * SIDE, FB):
            owner, first = row_block % GRID, 2 if row_block >= GRID else 0
            line = (row_block - LB) * SLICE - start
            for n in range(2 * pair, 2 * pair + 2):
                if first + n >= OUT_SLOTS or (first == 0 and n >= 2):
                    continue
                below = jnp.maximum(row_block - LB - y - SIDE * n, 0)
                slot = (TB - y) * n - 2 * n * (n - 1) + below
                tiles = sums[pl.ds(slot, SLICE, stride=TSLOTS), :]
                col = (n - 2 * pair) * BLOCK
                out[owner, first + n] = tiles - value[line : line + SLICE, col : col + BLOCK]


def product(position, along_x, along_y, sums):
    return pl.pallas_call(
        product_kernel,
        out_shape=[
            jax.ShapeDtypeStruct((GRID, OUT_SLOTS, SLICE, BLOCK), jnp.float32),
            jax.ShapeDtypeStruct((2, BLOCK, LEAD), jnp.float32),
        ],
        in_specs=[SMEM] + [VMEM] * 11,
        out_specs=[VMEM] * 2,
        scratch_shapes=[
            pltpu.VMEM((LINES * BLOCK, LEAD), jnp.bfloat16),
            pltpu.VMEM((LINES * BLOCK, LEAD), jnp.bfloat16),
            pltpu.VMEM((LINES * BLOCK, LEAD), jnp.bfloat16),
            pltpu.VMEM((LINES * BLOCK, LEAD), jnp.bfloat16),
        ],
        compiler_params=pltpu.CompilerParams(vmem_limit_bytes=VMEM_LIMIT),
        cost_estimate=pl.CostEstimate(flops=11 * 10**9, bytes_accessed=8 << 20, transcendentals=0),
        name="product",
    )(position, *along_x, *along_y, sums)


def lower(values, row_block, block, first_row):
    row = lax.broadcasted_iota(jnp.int32, values.shape, 0)
    col = lax.broadcasted_iota(jnp.int32, values.shape, 1)
    inside = block * BLOCK + col <= row_block * BLOCK + first_row + row
    return jnp.where(inside, values, 0.0)


def base_kernel(position, entries, lead_rows, own, out):
    g = position[0] * SIDE + position[1]
    out[0, :, :LEAD] = jnp.where(g < LB, lead_rows[...], own[0])
    out[1, :, :LEAD] = own[1]
    for local in range(2):
        for block in range(LB, FB):
            at = slice(block * BLOCK, (block + 1) * BLOCK)
            out[local, :, at] = lower(entries[local, :, at], local * GRID + g, block, 0)


def base(position, entries, lead_rows, own):
    return pl.pallas_call(
        base_kernel,
        out_shape=jax.ShapeDtypeStruct(entries.shape, jnp.float32),
        in_specs=[SMEM] + [VMEM] * 3,
        out_specs=VMEM,
        compiler_params=pltpu.CompilerParams(vmem_limit_bytes=VMEM_LIMIT),
        cost_estimate=pl.CostEstimate(flops=0, bytes_accessed=32 << 20, transcendentals=0),
        name="base",
    )(position, entries, lead_rows, own)


def finish_kernel(position, before, change, out):
    g = position[0] * SIDE + position[1]
    out[...] = before[...]
    for local in range(2):
        for block in range(LB, FB if local else GRID):
            at = slice(block * BLOCK, (block + 1) * BLOCK)
            y, n = block % SIDE, (block - LB) // SIDE
            for x in range(SIDE):
                span = slice(x * SLICE, (x + 1) * SLICE)
                value = lower(
                    change[x * SIDE + y, 2 * local + n], local * GRID + g, block, x * SLICE
                )
                out[local, span, at] = before[local, span, at] + value


def finish(position, before, change):
    return pl.pallas_call(
        finish_kernel,
        out_shape=jax.ShapeDtypeStruct(before.shape, jnp.float32),
        in_specs=[SMEM, VMEM, VMEM],
        out_specs=VMEM,
        compiler_params=pltpu.CompilerParams(vmem_limit_bytes=VMEM_LIMIT),
        name="finish",
    )(position, before, change)


def destination_bins(owners, local_rows, picks):
    front, g = owners // GRID, owners % GRID
    shifted = local_rows + (local_rows * GRID + g < LB).astype(jnp.int32)
    row_block = shifted * GRID + g
    col_block = picks % (row_block + 1)
    panel = (row_block % SIDE * FRONTS + front) * PSLOTS + (row_block - LB) // SIDE * LB + col_block
    y, n = col_block % SIDE, (col_block - LB) // SIDE
    slot = (TB - y) * n - 2 * n * (n - 1) + row_block - col_block
    trail = PBINS + (y * FRONTS + front) * TSLOTS + slot
    return jnp.where(col_block < LB, panel, trail)


def across(values, axes):
    return lax.all_to_all(values, axes, split_axis=0, concat_axis=0)


def local(front_entries, child_tiles, tile_owner, tile_rows, tile_picks):
    x, y, f = lax.axis_index("x"), lax.axis_index("y"), lax.axis_index("front")
    position = jnp.stack([x, y, f]).astype(jnp.int32)
    entries = front_entries[0, :, 0]
    half = BLOCK // 2
    lead = entries[0, :, :LEAD]
    other = lax.ppermute(lead[half:], "x", [(0, 2), (1, 3)])
    lead = jnp.where(x < 2, lead[:half], other).reshape(SLABS // 2, SUB, LEAD)
    bins = destination_bins(tile_owner[0, :, 0], tile_rows[0], tile_picks[0])
    bins = gather_front(bins).reshape(1, 1, LEAD).astype(jnp.float32)
    bins = jnp.pad(bins, ((0, 0), (0, SUB - 1), (0, 0)))
    lead, bins, tiles = lax.optimization_barrier((lead, bins, child_tiles))
    half = SLABS // 4
    lines, near, far, tiles = gather_lines(
        jnp.concatenate([lead[:half], bins], 0), lead[half:], tiles, turn
    )
    tiles, near, entries = lax.optimization_barrier((tiles, near, entries))
    lead = [piece for ring in zip(lines, near, far) for piece in ring_pieces(*ring)]
    rows = across(tiles, ("x", "y", "front")).reshape(-1, BLOCK)
    panel = entries[:, :, :LEAD].reshape(2, SIDE, SLICE, LEAD)
    panel = [
        lax.dynamic_index_in_dim(panel, (x + n) % SIDE, 1, keepdims=False) for n in range(SIDE)
    ]
    panel = [part if n == 0 else shift(part, "x", n) for n, part in enumerate(panel)]
    lead_rows, *inverse, bins = factor(position, lead)
    panel_sums, trail_sums = combine(position, bins.reshape(-1), rows)
    panel_sums = across(panel_sums.reshape(SLICE, PSLOTS, BLOCK), ("y", "front"))
    panel_sums, trail_sums = lax.optimization_barrier((panel_sums, trail_sums))
    trail_sums = across(trail_sums.reshape(SLICE, TSLOTS, BLOCK), ("y", "front"))
    solved = solve(position, panel, panel_sums.reshape(-1, BLOCK), *inverse)
    near = [ring_near(solved, axis) for axis in ("x", "y")]
    far = [ring_far(pair, axis) for pair, axis in zip(near, ("x", "y"))]
    along = [ring_pieces(solved, *pair) for pair in zip(near, far)]
    change, own = product(position, *along, trail_sums.reshape(-1, BLOCK))
    change = across(change, ("x", "y"))
    out = finish(position, base(position, entries, lead_rows, own), change)
    return out[None, :, None]


def solution(mesh):
    mesh = Mesh(mesh.devices.reshape(FRONTS, SIDE, SIDE), ("front", "x", "y"))
    grid = ("x", "y")
    return jax.shard_map(
        local,
        mesh=mesh,
        in_specs=(
            P("front", None, grid, None, None),
            P("front", grid, None, None),
            P("front", grid, None),
            P("front", grid),
            P("front", grid),
        ),
        out_specs=P("front", None, grid, None, None),
        check_vma=False,
    )
```

```python
import functools
import jax
import jax.numpy as jnp
from jax import lax
from jax.experimental import pallas as pl
from jax.experimental.pallas import tpu as pltpu
from jax.sharding import Mesh
from jax.sharding import PartitionSpec as P

BLOCK = 128
LEAD = 1024
LB = LEAD // BLOCK
FRONTS = 8
GRID = 16
SIDE = 4
DEVICES = FRONTS * GRID
FB = 32
TB = FB - LB
TILES = 128
LINES = TB // SIDE
SLICE = BLOCK // SIDE
PSLOTS = LINES * LB
TSLOTS = 88
SLOTS = PSLOTS + TSLOTS
BINS = SIDE * FRONTS * SLOTS
OUT_SLOTS = 2 + LINES
WIDE = 2 * BLOCK
PACKED = [WIDE * (c * (c + 1) // 2) for c in range(LEAD // WIDE + 1)]
SUB = 8
SLABS = BLOCK // SUB
ACCS = 8
VMEM_LIMIT = 60 << 20

highest = lax.Precision.HIGHEST
ANY = pl.BlockSpec(memory_space=pl.ANY)
VMEM = pl.BlockSpec(memory_space=pltpu.VMEM)
SMEM = pl.BlockSpec(memory_space=pltpu.SMEM)


def split(values):
    high = values.astype(jnp.bfloat16)
    return high, (values - high.astype(jnp.float32)).astype(jnp.bfloat16)


def mul(a, b):
    return lax.dot_general(a, b, (((1,), (1,)), ((), ())), preferred_element_type=jnp.float32)


def tdot(a, b):
    return lax.dot_general(
        a, b, (((0,), (0,)), ((), ())), precision=highest, preferred_element_type=jnp.float32
    )


def shift(block, axis, step):
    return lax.ppermute(block, axis, [(i, (i + step) % SIDE) for i in range(SIDE)])


def gather_front(values):
    others = [
        lax.ppermute(values, "front", [(i, i ^ k) for i in range(FRONTS)]) for k in range(1, FRONTS)
    ]
    return jnp.stack([values, *others])


def ring_near(block, axis):
    return shift(block, axis, -1), shift(block, axis, 1)


def ring_far(near, axis):
    from_next, from_prev = near
    half = from_prev.shape[0] // 2
    return shift(from_prev[:half], axis, 1), shift(from_next[half:], axis, -1)


def ring_pieces(block, near, far):
    return [block, near[0], *far, near[1]]


def gather_lines(first, second, given, work):
    lines = []
    for part, axis in ((first, "x"), (second, "y")):
        lines.append(jnp.stack([part, *(shift(part, axis, -n) for n in range(1, SIDE))]))
    lines, given = lax.optimization_barrier((lines, given))
    near = [ring_near(line, axis) for line, axis in zip(lines, ("y", "x"))]
    near, done = lax.optimization_barrier((near, work(given)))
    far = [ring_far(pair, axis) for pair, axis in zip(near, ("y", "x"))]
    return lines, near, far, done


def line_copies(pieces, place, sem, x, y):
    copies = []
    for h in range(2):
        own, nxt, far_a, far_b, prv = pieces[5 * h : 5 * h + 5]
        for outer in range(SIDE):
            for inner in range(SIDE):
                if outer == 2:
                    src = (far_a if inner < 2 else far_b).at[inner % 2]
                else:
                    src = (own, nxt, None, prv)[outer].at[inner]
                dx, dy = (inner, outer) if h == 0 else (outer, inner)
                for start, count, dst in place(h, (x + dx) % SIDE, (y + dy) % SIDE):
                    copies.append(
                        pltpu.make_async_copy(src.at[pl.ds(start, count)], dst, sem.at[len(copies)])
                    )
    return copies


def turn_kernel(x, out):
    tiles = out.shape[1]

    def body(i, carry):
        for first in range(0, tiles, SUB):
            rows = x[pl.ds(first * BLOCK + i, SUB, stride=BLOCK), :]
            out[i, first : first + SUB, :] = rows
        return carry

    lax.fori_loop(0, BLOCK, body, 0, unroll=4)


def turn(tiles):
    step = 64
    return pl.pallas_call(
        turn_kernel,
        grid=(TILES // step,),
        out_shape=jax.ShapeDtypeStruct((BLOCK, TILES, BLOCK), jnp.float32),
        in_specs=[pl.BlockSpec((step * BLOCK, BLOCK), lambda n: (n, 0))],
        out_specs=pl.BlockSpec((BLOCK, step, BLOCK), lambda n: (0, n, 0)),
        compiler_params=pltpu.CompilerParams(vmem_limit_bytes=VMEM_LIMIT),
        cost_estimate=pl.CostEstimate(flops=0, bytes_accessed=16 << 20, transcendentals=0),
        name="turn",
    )(tiles.reshape(TILES * BLOCK, BLOCK))


def combine_kernel(position, bins, x, out, *accs):
    sources = x.shape[0] // TILES

    @pl.when(pl.program_id(0) == 0)
    def _():
        for acc in accs:
            acc[...] = jnp.zeros_like(acc)

    def body(q, carry):
        source = (q // FRONTS) * FRONTS + jnp.bitwise_xor(q % FRONTS, position[2])
        base = pl.multiple_of(source * TILES, TILES)
        labels = (pl.program_id(0) * sources + q) * TILES
        for first in range(0, TILES, ACCS):
            at = [bins[labels + first + m] for m in range(ACCS)]
            rows = [x[pl.ds(base + first + m, 1), :] for m in range(ACCS)]
            sums = [accs[m][pl.ds(at[m], 1), :] + rows[m] for m in range(ACCS)]
            for m in range(ACCS):
                accs[m][pl.ds(at[m], 1), :] = sums[m]
        return carry

    lax.fori_loop(0, sources, body, 0)
    step = 256

    @pl.when(pl.program_id(0) == pl.num_programs(0) - 1)
    def _():
        def add(b, carry):
            at = pl.ds(pl.multiple_of(b * step, step), step)
            total = accs[0][at, :]
            for acc in accs[1:]:
                total = total + acc[at, :]
            out[at, :] = total
            return carry

        lax.fori_loop(0, BINS // step, add, 0)


def combine(position, bins, rows):
    steps = 4
    return pl.pallas_call(
        combine_kernel,
        grid=(steps,),
        out_shape=jax.ShapeDtypeStruct((BINS, BLOCK), jnp.float32),
        in_specs=[SMEM, SMEM, pl.BlockSpec((rows.shape[0] // steps, BLOCK), lambda i: (i, 0))],
        out_specs=pl.BlockSpec((BINS, BLOCK), lambda i: (0, 0)),
        scratch_shapes=[pltpu.VMEM((BINS, BLOCK), jnp.float32)] * ACCS,
        compiler_params=pltpu.CompilerParams(vmem_limit_bytes=VMEM_LIMIT),
        cost_estimate=pl.CostEstimate(flops=20 * 10**9, bytes_accessed=20 << 20, transcendentals=0),
        name="combine",
    )(position, bins, rows)


def factor_rows(rows, first, sub):
    def spread(values, j):
        return jnp.broadcast_to(values[j : j + 1, :], values.shape)

    columns = [
        jnp.broadcast_to(rows[:, first + j : first + j + 1], (SUB, BLOCK)) for j in range(SUB)
    ]
    parts = [rows[:, :BLOCK], rows[:, BLOCK:]]
    for j in range(SUB):
        scale = lax.rsqrt(spread(columns[j], j))
        weight = jnp.where(sub > j, columns[j] * scale, 0.0)
        for m in range(j + 1, SUB):
            columns[m] = columns[m] - weight * (spread(columns[m], j) * scale)
        for n in range(2):
            pivot = spread(parts[n], j) * scale
            parts[n] = jnp.where(sub == j, pivot, parts[n] - weight * pivot)
    return jnp.concatenate(parts, 1)


def factor_kernel(position, *refs):
    pieces, outs, scratch = refs[:10], refs[10:13], refs[13:]
    own_rows, inverse, labels = outs
    (entries, labels_in, work, diag, pair, sem) = scratch
    px, py = position[0], position[1]

    def place(h, x, y):
        block = (x % 2) * SIDE + y
        slab = block * SLABS + (x // 2) * (SLABS // 2) + h * (SLABS // 4)
        spans = [(0, SLABS // 4, entries.at[pl.ds(slab, SLABS // 4)])]
        if h == 0:
            spans.append((SLABS // 4, 1, labels_in.at[pl.ds(x * SIDE + y, 1)]))
        return spans

    copies = line_copies(pieces, place, sem, px, py)
    for copy in copies:
        copy.start()
    for copy in copies:
        copy.wait()
    for g in range(GRID):
        labels[g : g + 1, :] = labels_in[g, 0:1, :].astype(jnp.int32)
    sub = lax.broadcasted_iota(jnp.int32, (SUB, 1), 0)
    row = lax.broadcasted_iota(jnp.int32, (BLOCK, BLOCK), 0)
    col = lax.broadcasted_iota(jnp.int32, (BLOCK, BLOCK), 1)
    eye = jnp.where(row == col, 1.0, 0.0)
    for r in range(LB):
        for c in range(r + 1):
            block = entries[r * SLABS : (r + 1) * SLABS, :, c * BLOCK : (c + 1) * BLOCK]
            block = block.reshape(BLOCK, BLOCK)
            if r == c:
                block = jnp.where(col <= row, block, 0.0)
                block = block + jnp.where(col < row, block, 0.0).T
                work[r * BLOCK : (r + 1) * BLOCK, r * BLOCK : (r + 1) * BLOCK] = block
            else:
                work[c * BLOCK : (c + 1) * BLOCK, r * BLOCK : (r + 1) * BLOCK] = block.T

    def step(k, carry):
        at = pl.ds(pl.multiple_of(k * BLOCK, BLOCK), BLOCK)
        pair[:, :BLOCK] = work[at, at]
        pair[:, BLOCK:] = eye
        for q in range(BLOCK // SUB):
            first = SUB * q
            rows = pair[first : first + SUB, :]
            if q > 0:
                rows = rows - tdot(pair[0:first, first : first + SUB], pair[0:first, :])
            pair[first : first + SUB, :] = factor_rows(rows, first, sub)
        block_inverse = pair[:, BLOCK:]
        diag[k] = pair[:, :BLOCK]
        work[at, :] = jnp.dot(
            block_inverse, work[at, :], precision=highest, preferred_element_type=jnp.float32
        )
        work[at, at] = block_inverse

        def update(i, inner):
            below = pl.ds(pl.multiple_of(i * BLOCK, BLOCK), BLOCK)
            work[below, at] = jnp.zeros((BLOCK, BLOCK), jnp.float32)
            work[below, :] = work[below, :] - tdot(work[at, below], work[at, :])
            return inner

        lax.fori_loop(k + 1, LB, update, 0)
        return carry

    lax.fori_loop(0, LB, step, 0)
    for k in range(LB):
        at = slice(k * BLOCK, (k + 1) * BLOCK)
        start, width = PACKED[k // 2], (k + 1) * BLOCK
        part = slice(k % 2 * BLOCK, (k % 2 + 1) * BLOCK)
        high, low = split(work[at, :width])
        inverse[0, part, start : start + width] = high
        inverse[1, part, start : start + width] = low
        if k % 2 == 0:
            rest = jnp.zeros((2, BLOCK, BLOCK), jnp.bfloat16)
            inverse[:, part, start + width : start + width + BLOCK] = rest
    mine = jnp.minimum(px * SIDE + py, LB - 1)
    mine_at = pl.ds(pl.multiple_of(mine * BLOCK, BLOCK), BLOCK)
    for k in range(LB):
        at = slice(k * BLOCK, (k + 1) * BLOCK)
        block = jnp.where(k == mine, jnp.where(row <= col, diag[k], 0.0), work[at, mine_at])
        own_rows[:, at] = jnp.where(k <= mine, block, 0.0).T


def factor(position, pieces):
    return pl.pallas_call(
        factor_kernel,
        out_shape=[
            jax.ShapeDtypeStruct((BLOCK, LEAD), jnp.float32),
            jax.ShapeDtypeStruct((2, WIDE, PACKED[-1]), jnp.bfloat16),
            jax.ShapeDtypeStruct((GRID, LEAD), jnp.int32),
        ],
        in_specs=[SMEM] + [ANY] * 10,
        out_specs=[VMEM] * 3,
        scratch_shapes=[
            pltpu.VMEM((LB * SLABS, SUB, LEAD), jnp.float32),
            pltpu.VMEM((GRID, SUB, LEAD), jnp.float32),
            pltpu.VMEM((LEAD, LEAD), jnp.float32),
            pltpu.VMEM((LB, BLOCK, BLOCK), jnp.float32),
            pltpu.VMEM((BLOCK, 2 * BLOCK), jnp.float32),
            pltpu.SemaphoreType.DMA((48,)),
        ],
        compiler_params=pltpu.CompilerParams(vmem_limit_bytes=VMEM_LIMIT),
        cost_estimate=pl.CostEstimate(flops=120 * 10**9, bytes_accessed=20 << 20, transcendentals=1024),
        name="factor",
    )(position, *pieces)


def solve_kernel(position, own, part1, part2, part3, sums, inverse, out, rows):
    x = position[0]
    for step, part in enumerate((own, part1, part2, part3)):
        source = (x + SIDE - step) % SIDE
        for l in range(2):
            rows[SIDE * l + source] = part[l]
    for m in range(LINES):
        for c in range(LB):
            at = slice(c * BLOCK, (c + 1) * BLOCK)
            values = sums[pl.ds(m * LB + c, SLICE, stride=SLOTS), :]
            rows[LB // SIDE + m, :, at] = rows[LB // SIDE + m, :, at] + values
    high, low = split(rows[LB // SIDE :].reshape(LINES * SLICE, LEAD))
    for c in range(LEAD // WIDE):
        end = (c + 1) * WIDE
        inv_high, inv_low = inverse[:, :, PACKED[c] : PACKED[c + 1]]
        value = mul(high[:, :end], inv_high) + (
            mul(high[:, :end], inv_low) + mul(low[:, :end], inv_high)
        )
        out[:, :, end - WIDE : end] = value.reshape(LINES, SLICE, WIDE)


def solve(position, parts, sums, inverse):
    return pl.pallas_call(
        solve_kernel,
        out_shape=jax.ShapeDtypeStruct((LINES, SLICE, LEAD), jnp.float32),
        in_specs=[SMEM] + [VMEM] * 6,
        out_specs=VMEM,
        scratch_shapes=[pltpu.VMEM((2 * SIDE, SLICE, LEAD), jnp.float32)],
        compiler_params=pltpu.CompilerParams(vmem_limit_bytes=20 << 20),
        name="solve",
    )(position, *parts, sums, inverse)


def product_kernel(position, *refs):
    along_x, along_y, scratch = refs[:5], refs[5:10], refs[10:]
    sums, out, own, high, low, row_high, row_low = scratch
    x, y = position[0], position[1]
    half = LINES // 2
    out[...] = jnp.zeros_like(out)

    def blocks(pieces, here):
        nearby, nxt, far_a, far_b, prv = pieces
        for step, piece, first in (
            (0, nearby, 0),
            (1, nxt, 0),
            (2, far_a, 0),
            (2, far_b, half),
            (3, prv, 0),
        ):
            for m in range(piece.shape[0]):
                yield (here + step) % SIDE, first + m, piece[m]

    for index, m, values in blocks(along_x, x):
        at = pl.ds(pl.multiple_of(m * BLOCK + index * SLICE, SLICE), SLICE)
        high[at, :], low[at, :] = split(values)
    for l in range(2):
        m = jnp.maximum(x - 2, 0) if l == 0 else x + 2
        nearby, nxt, far_a, far_b, prv = along_x
        for step in range(SIDE):
            at = pl.ds(pl.multiple_of((x + step) % SIDE * SLICE, SLICE), SLICE)
            if step == 2:
                first = far_a[jnp.minimum(m, half - 1)]
                second = far_b[jnp.maximum(m - half, 0)]
                own[l, at, :] = jnp.where(m < half, first, second)
            else:
                own[l, at, :] = (nearby, nxt, None, prv)[step][m]
    for z, m, values in blocks(along_y, y):
        at = pl.ds(pl.multiple_of(m * BLOCK + z * SLICE, SLICE), SLICE)
        row_high[at, :], row_low[at, :] = split(values)
    for pair in range(LINES // 2):
        start = pair * 2 * BLOCK
        rows_high, rows_low = row_high[start:], row_low[start:]
        cols_high, cols_low = high[start : start + 2 * BLOCK], low[start : start + 2 * BLOCK]
        value = mul(rows_high, cols_high) + (mul(rows_high, cols_low) + mul(rows_low, cols_high))
        for row_block in range(LB + 2 * pair * SIDE, FB):
            owner, first = row_block % GRID, 2 if row_block >= GRID else 0
            line = (row_block - LB) * SLICE - start
            for n in range(2 * pair, 2 * pair + 2):
                if first + n >= OUT_SLOTS or (first == 0 and n >= 2):
                    continue
                below = jnp.maximum(row_block - LB - y - SIDE * n, 0)
                slot = (TB - y) * n - 2 * n * (n - 1) + below
                tiles = sums[pl.ds(PSLOTS + slot, SLICE, stride=SLOTS), :]
                col = (n - 2 * pair) * BLOCK
                out[owner, first + n] = tiles - value[line : line + SLICE, col : col + BLOCK]


def product(position, along_x, along_y, sums):
    return pl.pallas_call(
        product_kernel,
        out_shape=[
            jax.ShapeDtypeStruct((GRID, OUT_SLOTS, SLICE, BLOCK), jnp.float32),
            jax.ShapeDtypeStruct((2, BLOCK, LEAD), jnp.float32),
        ],
        in_specs=[SMEM] + [VMEM] * 11,
        out_specs=[VMEM] * 2,
        scratch_shapes=[
            pltpu.VMEM((LINES * BLOCK, LEAD), jnp.bfloat16),
            pltpu.VMEM((LINES * BLOCK, LEAD), jnp.bfloat16),
            pltpu.VMEM((LINES * BLOCK, LEAD), jnp.bfloat16),
            pltpu.VMEM((LINES * BLOCK, LEAD), jnp.bfloat16),
        ],
        compiler_params=pltpu.CompilerParams(vmem_limit_bytes=32 << 20),
        cost_estimate=pl.CostEstimate(flops=11 * 10**9, bytes_accessed=8 << 20, transcendentals=0),
        name="product",
    )(position, *along_x, *along_y, sums)


def lower(values, row_block, block, first_row):
    row = lax.broadcasted_iota(jnp.int32, values.shape, 0)
    col = lax.broadcasted_iota(jnp.int32, values.shape, 1)
    inside = block * BLOCK + col <= row_block * BLOCK + first_row + row
    return jnp.where(inside, values, 0.0)


def base_kernel(position, lead_rows, own, out):
    g = position[0] * SIDE + position[1]
    out[0, :, :LEAD] = jnp.where(g < LB, lead_rows[...], own[0])
    out[1, :, :LEAD] = own[1]
    out[:, :, LEAD:] = jnp.zeros((2, BLOCK, TB * BLOCK), jnp.float32)


def base(position, shape, lead_rows, own):
    return pl.pallas_call(
        base_kernel,
        out_shape=jax.ShapeDtypeStruct(shape, jnp.float32),
        in_specs=[SMEM, VMEM, VMEM],
        out_specs=VMEM,
        compiler_params=pltpu.CompilerParams(vmem_limit_bytes=16 << 20),
        cost_estimate=pl.CostEstimate(flops=0, bytes_accessed=32 << 20, transcendentals=0),
        name="base",
    )(position, lead_rows, own)


def finish_kernel(position, before, entries_in, change_in, out, entries, change, values, sem):
    g = position[0] * SIDE + position[1]
    wide = SIDE * BLOCK
    steps = [(0, n) for n in range(2)] + [(1, n) for n in range(LINES)]
    arriving, leaving = [], []
    for i, (local, n) in enumerate(steps):
        at = pl.ds(LEAD + n * wide, wide)
        arriving.append(
            (
                pltpu.make_async_copy(entries_in.at[local, :, at], entries.at[i], sem.at[0, i]),
                pltpu.make_async_copy(change_in.at[:, i], change.at[i], sem.at[1, i]),
            )
        )
        leaving.append(pltpu.make_async_copy(values.at[i], out.at[local, :, at], sem.at[2, i]))
    for pair in arriving:
        for copy in pair:
            copy.start()
    for i, (local, n) in enumerate(steps):
        for copy in arriving[i]:
            copy.wait()
        for y in range(SIDE):
            at = slice(y * BLOCK, (y + 1) * BLOCK)
            for x in range(SIDE):
                span = slice(x * SLICE, (x + 1) * SLICE)
                value = entries[i, span, at] + change[i, x * SIDE + y]
                block = LB + n * SIDE + y
                values[i, span, at] = lower(value, local * GRID + g, block, x * SLICE)
        leaving[i].start()
    for copy in leaving:
        copy.wait()


def finish(position, before, entries, change):
    return pl.pallas_call(
        finish_kernel,
        out_shape=jax.ShapeDtypeStruct(before.shape, jnp.float32),
        in_specs=[SMEM, ANY, ANY, ANY],
        out_specs=ANY,
        input_output_aliases={1: 0},
        scratch_shapes=[
            pltpu.VMEM((OUT_SLOTS, BLOCK, SIDE * BLOCK), jnp.float32),
            pltpu.VMEM((OUT_SLOTS, GRID, SLICE, BLOCK), jnp.float32),
            pltpu.VMEM((OUT_SLOTS, BLOCK, SIDE * BLOCK), jnp.float32),
            pltpu.SemaphoreType.DMA((3, OUT_SLOTS)),
        ],
        compiler_params=pltpu.CompilerParams(vmem_limit_bytes=VMEM_LIMIT),
        name="finish",
    )(position, before, entries, change)


def destination_bins(owners, local_rows, picks):
    front, g = owners // GRID, owners % GRID
    shifted = local_rows + (local_rows * GRID + g < LB).astype(jnp.int32)
    row_block = shifted * GRID + g
    col_block = picks % (row_block + 1)
    panel = (row_block % SIDE * FRONTS + front) * SLOTS + (row_block - LB) // SIDE * LB + col_block
    y, n = col_block % SIDE, (col_block - LB) // SIDE
    slot = (TB - y) * n - 2 * n * (n - 1) + row_block - col_block
    trail = (y * FRONTS + front) * SLOTS + PSLOTS + slot
    return jnp.where(col_block < LB, panel, trail)


def across(values, axes):
    return lax.all_to_all(values, axes, split_axis=0, concat_axis=0)


def local(front_entries, child_tiles, tile_owner, tile_rows, tile_picks):
    x, y, f = lax.axis_index("x"), lax.axis_index("y"), lax.axis_index("front")
    position = jnp.stack([x, y, f]).astype(jnp.int32)
    entries = front_entries[0, :, 0]
    half = BLOCK // 2
    lead = entries[0, :, :LEAD]
    other = lax.ppermute(lead[half:], "x", [(0, 2), (1, 3)])
    lead = jnp.where(x < 2, lead[:half], other).reshape(SLABS // 2, SUB, LEAD)
    bins = destination_bins(tile_owner[0, :, 0], tile_rows[0], tile_picks[0])
    bins = gather_front(bins).reshape(1, 1, LEAD).astype(jnp.float32)
    bins = jnp.pad(bins, ((0, 0), (0, SUB - 1), (0, 0)))
    lead, bins, tiles = lax.optimization_barrier((lead, bins, child_tiles))
    half = SLABS // 4
    lines, near, far, tiles = gather_lines(
        jnp.concatenate([lead[:half], bins], 0), lead[half:], tiles, turn
    )
    tiles, near, entries = lax.optimization_barrier((tiles, near, entries))
    lead = [piece for ring in zip(lines, near, far) for piece in ring_pieces(*ring)]
    rows = across(tiles, ("x", "y", "front")).reshape(-1, BLOCK)
    panel = entries[:, :, :LEAD].reshape(2, SIDE, SLICE, LEAD)
    panel = [
        lax.dynamic_index_in_dim(panel, (x + n) % SIDE, 1, keepdims=False) for n in range(SIDE)
    ]
    panel = [part if n == 0 else shift(part, "x", n) for n, part in enumerate(panel)]
    lead_rows, inverse, bins = factor(position, lead)
    sums = combine(position, bins.reshape(-1), rows).reshape(SLICE, SLOTS, BLOCK)
    sums = across(sums, ("y", "front")).reshape(-1, BLOCK)
    solved = solve(position, panel, sums, inverse)
    near = [ring_near(solved, axis) for axis in ("x", "y")]
    far = [ring_far(pair, axis) for pair, axis in zip(near, ("x", "y"))]
    along = [ring_pieces(solved, *pair) for pair in zip(near, far)]
    change, own = product(position, *along, sums)
    change = across(change, ("x", "y"))
    out = finish(position, base(position, entries.shape, lead_rows, own), entries, change)
    return out[None, :, None]


def solution(mesh):
    mesh = Mesh(mesh.devices.reshape(FRONTS, SIDE, SIDE), ("front", "x", "y"))
    grid = ("x", "y")
    return jax.shard_map(
        local,
        mesh=mesh,
        in_specs=(
            P("front", None, grid, None, None),
            P("front", grid, None, None),
            P("front", grid, None),
            P("front", grid),
            P("front", grid),
        ),
        out_specs=P("front", None, grid, None, None),
        check_vma=False,
    )
```

```python
import functools
import jax
import jax.numpy as jnp
from jax import lax
from jax.experimental import pallas as pl
from jax.experimental.pallas import tpu as pltpu
from jax.sharding import Mesh
from jax.sharding import PartitionSpec as P

BLOCK = 128
LEAD = 1024
LB = LEAD // BLOCK
FRONTS = 8
GRID = 16
SIDE = 4
DEVICES = FRONTS * GRID
FB = 32
TB = FB - LB
TILES = 128
LINES = TB // SIDE
SLICE = BLOCK // SIDE
PSLOTS = LINES * LB
TSLOTS = 88
SLOTS = PSLOTS + TSLOTS
BINS = SIDE * FRONTS * SLOTS
OUT_SLOTS = 2 + LINES
WIDE = 2 * BLOCK
PACKED = [WIDE * (c * (c + 1) // 2) for c in range(LEAD // WIDE + 1)]
SUB = 8
SLABS = BLOCK // SUB
ACCS = 8
VMEM_LIMIT = 60 << 20

highest = lax.Precision.HIGHEST
ANY = pl.BlockSpec(memory_space=pl.ANY)
VMEM = pl.BlockSpec(memory_space=pltpu.VMEM)
SMEM = pl.BlockSpec(memory_space=pltpu.SMEM)


def split(values):
    high = values.astype(jnp.bfloat16)
    return high, (values - high.astype(jnp.float32)).astype(jnp.bfloat16)


def mul(a, b):
    return lax.dot_general(a, b, (((1,), (1,)), ((), ())), preferred_element_type=jnp.float32)


def tdot(a, b):
    return lax.dot_general(
        a, b, (((0,), (0,)), ((), ())), precision=highest, preferred_element_type=jnp.float32
    )


def shift(block, axis, step):
    return lax.ppermute(block, axis, [(i, (i + step) % SIDE) for i in range(SIDE)])


def gather_front(values):
    others = [
        lax.ppermute(values, "front", [(i, i ^ k) for i in range(FRONTS)]) for k in range(1, FRONTS)
    ]
    return jnp.stack([values, *others])


def ring_near(block, axis):
    return shift(block, axis, -1), shift(block, axis, 1)


def ring_far(near, axis):
    from_next, from_prev = near
    half = from_prev.shape[0] // 2
    return shift(from_prev[:half], axis, 1), shift(from_next[half:], axis, -1)


def ring_pieces(block, near, far):
    return [block, near[0], *far, near[1]]


def gather_lines(first, second, given, work):
    lines = []
    for part, axis in ((first, "x"), (second, "y")):
        lines.append(jnp.stack([part, *(shift(part, axis, -n) for n in range(1, SIDE))]))
    lines, given = lax.optimization_barrier((lines, given))
    near = [ring_near(line, axis) for line, axis in zip(lines, ("y", "x"))]
    near, done = lax.optimization_barrier((near, work(given)))
    far = [ring_far(pair, axis) for pair, axis in zip(near, ("y", "x"))]
    return lines, near, far, done


def line_copies(pieces, place, sem, x, y):
    copies = []
    for h in range(2):
        own, nxt, far_a, far_b, prv = pieces[5 * h : 5 * h + 5]
        for outer in range(SIDE):
            for inner in range(SIDE):
                if outer == 2:
                    src = (far_a if inner < 2 else far_b).at[inner % 2]
                else:
                    src = (own, nxt, None, prv)[outer].at[inner]
                dx, dy = (inner, outer) if h == 0 else (outer, inner)
                for start, count, dst in place(h, (x + dx) % SIDE, (y + dy) % SIDE):
                    copies.append(
                        pltpu.make_async_copy(src.at[pl.ds(start, count)], dst, sem.at[len(copies)])
                    )
    return copies


def turn_kernel(x, out):
    tiles = out.shape[1]

    def body(i, carry):
        for first in range(0, tiles, SUB):
            rows = x[pl.ds(first * BLOCK + i, SUB, stride=BLOCK), :]
            out[i, first : first + SUB, :] = rows
        return carry

    lax.fori_loop(0, BLOCK, body, 0, unroll=4)


def turn(tiles):
    step = 64
    return pl.pallas_call(
        turn_kernel,
        grid=(TILES // step,),
        out_shape=jax.ShapeDtypeStruct((BLOCK, TILES, BLOCK), jnp.float32),
        in_specs=[pl.BlockSpec((step * BLOCK, BLOCK), lambda n: (n, 0))],
        out_specs=pl.BlockSpec((BLOCK, step, BLOCK), lambda n: (0, n, 0)),
        compiler_params=pltpu.CompilerParams(vmem_limit_bytes=VMEM_LIMIT),
        cost_estimate=pl.CostEstimate(flops=0, bytes_accessed=16 << 20, transcendentals=0),
        name="turn",
    )(tiles.reshape(TILES * BLOCK, BLOCK))


def combine_kernel(position, bins, x, out, *accs):
    sources = x.shape[0] // TILES

    @pl.when(pl.program_id(0) == 0)
    def _():
        for acc in accs:
            acc[...] = jnp.zeros_like(acc)

    def body(q, carry):
        line, k = q // FRONTS, q % FRONTS
        source = line * FRONTS + jnp.bitwise_xor(k, position[2])
        base = pl.multiple_of(source * TILES, TILES)
        labels = (k * GRID + pl.program_id(0) * (sources // FRONTS) + line) * TILES
        for first in range(0, TILES, ACCS):
            at = [bins[labels + first + m] for m in range(ACCS)]
            rows = [x[pl.ds(base + first + m, 1), :] for m in range(ACCS)]
            sums = [accs[m][pl.ds(at[m], 1), :] + rows[m] for m in range(ACCS)]
            for m in range(ACCS):
                accs[m][pl.ds(at[m], 1), :] = sums[m]
        return carry

    lax.fori_loop(0, sources, body, 0)
    step = 256

    @pl.when(pl.program_id(0) == pl.num_programs(0) - 1)
    def _():
        def add(b, carry):
            at = pl.ds(pl.multiple_of(b * step, step), step)
            total = accs[0][at, :]
            for acc in accs[1:]:
                total = total + acc[at, :]
            out[at, :] = total
            return carry

        lax.fori_loop(0, BINS // step, add, 0)


def combine(position, bins, rows):
    steps = 4
    return pl.pallas_call(
        combine_kernel,
        grid=(steps,),
        out_shape=jax.ShapeDtypeStruct((BINS, BLOCK), jnp.float32),
        in_specs=[SMEM, SMEM, pl.BlockSpec((rows.shape[0] // steps, BLOCK), lambda i: (i, 0))],
        out_specs=pl.BlockSpec((BINS, BLOCK), lambda i: (0, 0)),
        scratch_shapes=[pltpu.VMEM((BINS, BLOCK), jnp.float32)] * ACCS,
        compiler_params=pltpu.CompilerParams(vmem_limit_bytes=VMEM_LIMIT),
        cost_estimate=pl.CostEstimate(flops=20 * 10**9, bytes_accessed=20 << 20, transcendentals=0),
        name="combine",
    )(position, bins, rows)


def factor_rows(rows, first, sub):
    def spread(values, j):
        return jnp.broadcast_to(values[j : j + 1, :], values.shape)

    columns = [
        jnp.broadcast_to(rows[:, first + j : first + j + 1], (SUB, BLOCK)) for j in range(SUB)
    ]
    parts = [rows[:, :BLOCK], rows[:, BLOCK:]]
    for j in range(SUB):
        scale = lax.rsqrt(spread(columns[j], j))
        weight = jnp.where(sub > j, columns[j] * scale, 0.0)
        for m in range(j + 1, SUB):
            columns[m] = columns[m] - weight * (spread(columns[m], j) * scale)
        for n in range(2):
            pivot = spread(parts[n], j) * scale
            parts[n] = jnp.where(sub == j, pivot, parts[n] - weight * pivot)
    return jnp.concatenate(parts, 1)


def factor_kernel(position, *refs):
    pieces, outs, scratch = refs[:10], refs[10:13], refs[13:]
    own_rows, inverse, labels = outs
    (entries, labels_in, work, diag, pair, sem) = scratch
    px, py = position[0], position[1]

    def place(h, x, y):
        block = (x % 2) * SIDE + y
        slab = block * SLABS + (x // 2) * (SLABS // 2) + h * (SLABS // 4)
        spans = [(0, SLABS // 4, entries.at[pl.ds(slab, SLABS // 4)])]
        if h == 0:
            spans.append((SLABS // 4, 1, labels_in.at[pl.ds(x * SIDE + y, 1)]))
        return spans

    copies = line_copies(pieces, place, sem, px, py)
    for copy in copies:
        copy.start()
    for copy in copies:
        copy.wait()
    for g in range(GRID):
        labels[g : g + 1, :] = labels_in[g, 0:1, :TILES].astype(jnp.int32)
    sub = lax.broadcasted_iota(jnp.int32, (SUB, 1), 0)
    row = lax.broadcasted_iota(jnp.int32, (BLOCK, BLOCK), 0)
    col = lax.broadcasted_iota(jnp.int32, (BLOCK, BLOCK), 1)
    eye = jnp.where(row == col, 1.0, 0.0)
    for r in range(LB):
        for c in range(r + 1):
            block = entries[r * SLABS : (r + 1) * SLABS, :, c * BLOCK : (c + 1) * BLOCK]
            block = block.reshape(BLOCK, BLOCK)
            if r == c:
                block = jnp.where(col <= row, block, 0.0)
                block = block + jnp.where(col < row, block, 0.0).T
                work[r * BLOCK : (r + 1) * BLOCK, r * BLOCK : (r + 1) * BLOCK] = block
            else:
                work[c * BLOCK : (c + 1) * BLOCK, r * BLOCK : (r + 1) * BLOCK] = block.T

    def step(k, carry):
        at = pl.ds(pl.multiple_of(k * BLOCK, BLOCK), BLOCK)
        pair[:, :BLOCK] = work[at, at]
        pair[:, BLOCK:] = eye
        for q in range(BLOCK // SUB):
            first = SUB * q
            rows = pair[first : first + SUB, :]
            if q > 0:
                rows = rows - tdot(pair[0:first, first : first + SUB], pair[0:first, :])
            pair[first : first + SUB, :] = factor_rows(rows, first, sub)
        block_inverse = pair[:, BLOCK:]
        diag[k] = pair[:, :BLOCK]
        work[at, :] = jnp.dot(
            block_inverse, work[at, :], precision=highest, preferred_element_type=jnp.float32
        )
        work[at, at] = block_inverse

        def update(i, inner):
            below = pl.ds(pl.multiple_of(i * BLOCK, BLOCK), BLOCK)
            work[below, at] = jnp.zeros((BLOCK, BLOCK), jnp.float32)
            work[below, :] = work[below, :] - tdot(work[at, below], work[at, :])
            return inner

        lax.fori_loop(k + 1, LB, update, 0)
        return carry

    lax.fori_loop(0, LB, step, 0)
    for k in range(LB):
        at = slice(k * BLOCK, (k + 1) * BLOCK)
        start, width = PACKED[k // 2], (k + 1) * BLOCK
        part = slice(k % 2 * BLOCK, (k % 2 + 1) * BLOCK)
        high, low = split(work[at, :width])
        inverse[0, part, start : start + width] = high
        inverse[1, part, start : start + width] = low
        if k % 2 == 0:
            rest = jnp.zeros((2, BLOCK, BLOCK), jnp.bfloat16)
            inverse[:, part, start + width : start + width + BLOCK] = rest
    mine = jnp.minimum(px * SIDE + py, LB - 1)
    mine_at = pl.ds(pl.multiple_of(mine * BLOCK, BLOCK), BLOCK)
    for k in range(LB):
        at = slice(k * BLOCK, (k + 1) * BLOCK)
        block = jnp.where(k == mine, jnp.where(row <= col, diag[k], 0.0), work[at, mine_at])
        own_rows[:, at] = jnp.where(k <= mine, block, 0.0).T


def factor(position, pieces):
    return pl.pallas_call(
        factor_kernel,
        out_shape=[
            jax.ShapeDtypeStruct((BLOCK, LEAD), jnp.float32),
            jax.ShapeDtypeStruct((2, WIDE, PACKED[-1]), jnp.bfloat16),
            jax.ShapeDtypeStruct((GRID, TILES), jnp.int32),
        ],
        in_specs=[SMEM] + [ANY] * 10,
        out_specs=[VMEM] * 3,
        scratch_shapes=[
            pltpu.VMEM((LB * SLABS, SUB, LEAD), jnp.float32),
            pltpu.VMEM((GRID, SUB, LEAD), jnp.float32),
            pltpu.VMEM((LEAD, LEAD), jnp.float32),
            pltpu.VMEM((LB, BLOCK, BLOCK), jnp.float32),
            pltpu.VMEM((BLOCK, 2 * BLOCK), jnp.float32),
            pltpu.SemaphoreType.DMA((48,)),
        ],
        compiler_params=pltpu.CompilerParams(vmem_limit_bytes=VMEM_LIMIT),
        cost_estimate=pl.CostEstimate(flops=120 * 10**9, bytes_accessed=20 << 20, transcendentals=1024),
        name="factor",
    )(position, *pieces)


def solve_kernel(position, own, part1, part2, part3, sums, inverse, out, rows):
    x = position[0]
    for step, part in enumerate((own, part1, part2, part3)):
        source = (x + SIDE - step) % SIDE
        for l in range(2):
            rows[SIDE * l + source] = part[l]
    for m in range(LINES):
        for c in range(LB):
            at = slice(c * BLOCK, (c + 1) * BLOCK)
            values = sums[pl.ds(m * LB + c, SLICE, stride=SLOTS), :]
            rows[LB // SIDE + m, :, at] = rows[LB // SIDE + m, :, at] + values
    high, low = split(rows[LB // SIDE :].reshape(LINES * SLICE, LEAD))
    for c in range(LEAD // WIDE):
        end = (c + 1) * WIDE
        inv_high, inv_low = inverse[:, :, PACKED[c] : PACKED[c + 1]]
        value = mul(high[:, :end], inv_high) + (
            mul(high[:, :end], inv_low) + mul(low[:, :end], inv_high)
        )
        out[:, :, end - WIDE : end] = value.reshape(LINES, SLICE, WIDE)


def solve(position, parts, sums, inverse):
    return pl.pallas_call(
        solve_kernel,
        out_shape=jax.ShapeDtypeStruct((LINES, SLICE, LEAD), jnp.float32),
        in_specs=[SMEM] + [VMEM] * 6,
        out_specs=VMEM,
        scratch_shapes=[pltpu.VMEM((2 * SIDE, SLICE, LEAD), jnp.float32)],
        compiler_params=pltpu.CompilerParams(vmem_limit_bytes=20 << 20),
        name="solve",
    )(position, *parts, sums, inverse)


def product_kernel(position, *refs):
    along_x, along_y, scratch = refs[:5], refs[5:10], refs[10:]
    sums, out, own, high, low, row_high, row_low = scratch
    x, y = position[0], position[1]
    half = LINES // 2
    out[...] = jnp.zeros_like(out)

    def blocks(pieces, here):
        nearby, nxt, far_a, far_b, prv = pieces
        for step, piece, first in (
            (0, nearby, 0),
            (1, nxt, 0),
            (2, far_a, 0),
            (2, far_b, half),
            (3, prv, 0),
        ):
            for m in range(piece.shape[0]):
                yield (here + step) % SIDE, first + m, piece[m]

    for index, m, values in blocks(along_x, x):
        at = pl.ds(pl.multiple_of(m * BLOCK + index * SLICE, SLICE), SLICE)
        high[at, :], low[at, :] = split(values)
    for l in range(2):
        m = jnp.maximum(x - 2, 0) if l == 0 else x + 2
        nearby, nxt, far_a, far_b, prv = along_x
        for step in range(SIDE):
            at = pl.ds(pl.multiple_of((x + step) % SIDE * SLICE, SLICE), SLICE)
            if step == 2:
                first = far_a[jnp.minimum(m, half - 1)]
                second = far_b[jnp.maximum(m - half, 0)]
                own[l, at, :] = jnp.where(m < half, first, second)
            else:
                own[l, at, :] = (nearby, nxt, None, prv)[step][m]
    for z, m, values in blocks(along_y, y):
        at = pl.ds(pl.multiple_of(m * BLOCK + z * SLICE, SLICE), SLICE)
        row_high[at, :], row_low[at, :] = split(values)
    for pair in range(LINES // 2):
        start = pair * 2 * BLOCK
        rows_high, rows_low = row_high[start:], row_low[start:]
        cols_high, cols_low = high[start : start + 2 * BLOCK], low[start : start + 2 * BLOCK]
        value = mul(rows_high, cols_high) + (mul(rows_high, cols_low) + mul(rows_low, cols_high))
        for row_block in range(LB + 2 * pair * SIDE, FB):
            owner, first = row_block % GRID, 2 if row_block >= GRID else 0
            line = (row_block - LB) * SLICE - start
            for n in range(2 * pair, 2 * pair + 2):
                if first + n >= OUT_SLOTS or (first == 0 and n >= 2):
                    continue
                below = jnp.maximum(row_block - LB - y - SIDE * n, 0)
                slot = (TB - y) * n - 2 * n * (n - 1) + below
                tiles = sums[pl.ds(PSLOTS + slot, SLICE, stride=SLOTS), :]
                col = (n - 2 * pair) * BLOCK
                out[owner, first + n] = tiles - value[line : line + SLICE, col : col + BLOCK]


def product(position, along_x, along_y, sums):
    return pl.pallas_call(
        product_kernel,
        out_shape=[
            jax.ShapeDtypeStruct((GRID, OUT_SLOTS, SLICE, BLOCK), jnp.float32),
            jax.ShapeDtypeStruct((2, BLOCK, LEAD), jnp.float32),
        ],
        in_specs=[SMEM] + [VMEM] * 11,
        out_specs=[VMEM] * 2,
        scratch_shapes=[
            pltpu.VMEM((LINES * BLOCK, LEAD), jnp.bfloat16),
            pltpu.VMEM((LINES * BLOCK, LEAD), jnp.bfloat16),
            pltpu.VMEM((LINES * BLOCK, LEAD), jnp.bfloat16),
            pltpu.VMEM((LINES * BLOCK, LEAD), jnp.bfloat16),
        ],
        compiler_params=pltpu.CompilerParams(vmem_limit_bytes=32 << 20),
        cost_estimate=pl.CostEstimate(flops=11 * 10**9, bytes_accessed=8 << 20, transcendentals=0),
        name="product",
    )(position, *along_x, *along_y, sums)


def lower(values, row_block, block, first_row):
    row = lax.broadcasted_iota(jnp.int32, values.shape, 0)
    col = lax.broadcasted_iota(jnp.int32, values.shape, 1)
    inside = block * BLOCK + col <= row_block * BLOCK + first_row + row
    return jnp.where(inside, values, 0.0)


def base_kernel(position, lead_rows, own, out):
    g = position[0] * SIDE + position[1]
    out[0, :, :LEAD] = jnp.where(g < LB, lead_rows[...], own[0])
    out[1, :, :LEAD] = own[1]
    out[:, :, LEAD:] = jnp.zeros((2, BLOCK, TB * BLOCK), jnp.float32)


def base(position, shape, lead_rows, own):
    return pl.pallas_call(
        base_kernel,
        out_shape=jax.ShapeDtypeStruct(shape, jnp.float32),
        in_specs=[SMEM, VMEM, VMEM],
        out_specs=VMEM,
        compiler_params=pltpu.CompilerParams(vmem_limit_bytes=16 << 20),
        cost_estimate=pl.CostEstimate(flops=0, bytes_accessed=32 << 20, transcendentals=0),
        name="base",
    )(position, lead_rows, own)


def finish_kernel(position, before, entries_in, change_in, out, entries, change, values, sem):
    g = position[0] * SIDE + position[1]
    wide = SIDE * BLOCK
    steps = [(0, n) for n in range(2)] + [(1, n) for n in range(LINES)]
    arriving, leaving = [], []
    for i, (local, n) in enumerate(steps):
        at = pl.ds(LEAD + n * wide, wide)
        arriving.append(
            (
                pltpu.make_async_copy(entries_in.at[local, :, at], entries.at[i], sem.at[0, i]),
                pltpu.make_async_copy(change_in.at[:, i], change.at[i], sem.at[1, i]),
            )
        )
        leaving.append(pltpu.make_async_copy(values.at[i], out.at[local, :, at], sem.at[2, i]))
    for pair in arriving:
        for copy in pair:
            copy.start()
    for i, (local, n) in enumerate(steps):
        for copy in arriving[i]:
            copy.wait()
        for y in range(SIDE):
            at = slice(y * BLOCK, (y + 1) * BLOCK)
            for x in range(SIDE):
                span = slice(x * SLICE, (x + 1) * SLICE)
                value = entries[i, span, at] + change[i, x * SIDE + y]
                block = LB + n * SIDE + y
                values[i, span, at] = lower(value, local * GRID + g, block, x * SLICE)
        leaving[i].start()
    for copy in leaving:
        copy.wait()


def finish(position, before, entries, change):
    return pl.pallas_call(
        finish_kernel,
        out_shape=jax.ShapeDtypeStruct(before.shape, jnp.float32),
        in_specs=[SMEM, ANY, ANY, ANY],
        out_specs=ANY,
        input_output_aliases={1: 0},
        scratch_shapes=[
            pltpu.VMEM((OUT_SLOTS, BLOCK, SIDE * BLOCK), jnp.float32),
            pltpu.VMEM((OUT_SLOTS, GRID, SLICE, BLOCK), jnp.float32),
            pltpu.VMEM((OUT_SLOTS, BLOCK, SIDE * BLOCK), jnp.float32),
            pltpu.SemaphoreType.DMA((3, OUT_SLOTS)),
        ],
        compiler_params=pltpu.CompilerParams(vmem_limit_bytes=VMEM_LIMIT),
        name="finish",
    )(position, before, entries, change)


def destination_bins(owners, local_rows, picks):
    front, g = owners // GRID, owners % GRID
    shifted = local_rows + (local_rows * GRID + g < LB).astype(jnp.int32)
    row_block = shifted * GRID + g
    col_block = picks % (row_block + 1)
    panel = (row_block % SIDE * FRONTS + front) * SLOTS + (row_block - LB) // SIDE * LB + col_block
    y, n = col_block % SIDE, (col_block - LB) // SIDE
    slot = (TB - y) * n - 2 * n * (n - 1) + row_block - col_block
    trail = (y * FRONTS + front) * SLOTS + PSLOTS + slot
    return jnp.where(col_block < LB, panel, trail)


def across(values, axes):
    return lax.all_to_all(values, axes, split_axis=0, concat_axis=0)


def local(front_entries, child_tiles, tile_owner, tile_rows, tile_picks):
    x, y, f = lax.axis_index("x"), lax.axis_index("y"), lax.axis_index("front")
    position = jnp.stack([x, y, f]).astype(jnp.int32)
    entries = front_entries[0, :, 0]
    half = BLOCK // 2
    lead = entries[0, :, :LEAD]
    other = lax.ppermute(lead[half:], "x", [(0, 2), (1, 3)])
    lead = jnp.where(x < 2, lead[:half], other).reshape(SLABS // 2, SUB, LEAD)
    bins = destination_bins(tile_owner[0, :, 0], tile_rows[0], tile_picks[0])
    bins = jnp.pad(bins.astype(jnp.float32).reshape(1, 1, TILES), ((0, 0), (0, SUB - 1), (0, LEAD - TILES)))
    lead, bins, tiles = lax.optimization_barrier((lead, bins, child_tiles))
    half = SLABS // 4
    lines, near, far, tiles = gather_lines(
        jnp.concatenate([lead[:half], bins], 0), lead[half:], tiles, turn
    )
    tiles, near, entries = lax.optimization_barrier((tiles, near, entries))
    lead = [piece for ring in zip(lines, near, far) for piece in ring_pieces(*ring)]
    rows = across(tiles, ("x", "y", "front")).reshape(-1, BLOCK)
    panel = entries[:, :, :LEAD].reshape(2, SIDE, SLICE, LEAD)
    panel = [
        lax.dynamic_index_in_dim(panel, (x + n) % SIDE, 1, keepdims=False) for n in range(SIDE)
    ]
    panel = [part if n == 0 else shift(part, "x", n) for n, part in enumerate(panel)]
    lead_rows, inverse, bins = factor(position, lead)
    bins = gather_front(bins).reshape(-1)
    sums = combine(position, bins, rows).reshape(SLICE, SLOTS, BLOCK)
    sums = across(sums, ("y", "front")).reshape(-1, BLOCK)
    solved = solve(position, panel, sums, inverse)
    near = [ring_near(solved, axis) for axis in ("x", "y")]
    far = [ring_far(pair, axis) for pair, axis in zip(near, ("x", "y"))]
    along = [ring_pieces(solved, *pair) for pair in zip(near, far)]
    change, own = product(position, *along, sums)
    change = across(change, ("x", "y"))
    out = finish(position, base(position, entries.shape, lead_rows, own), entries, change)
    return out[None, :, None]


def solution(mesh):
    mesh = Mesh(mesh.devices.reshape(FRONTS, SIDE, SIDE), ("front", "x", "y"))
    grid = ("x", "y")
    return jax.shard_map(
        local,
        mesh=mesh,
        in_specs=(
            P("front", None, grid, None, None),
            P("front", grid, None, None),
            P("front", grid, None),
            P("front", grid),
            P("front", grid),
        ),
        out_specs=P("front", None, grid, None, None),
        check_vma=False,
    )
```

```python
import functools
import jax
import jax.numpy as jnp
from jax import lax
from jax.experimental import pallas as pl
from jax.experimental.pallas import tpu as pltpu
from jax.sharding import Mesh
from jax.sharding import PartitionSpec as P

BLOCK = 128
LEAD = 1024
LB = LEAD // BLOCK
FRONTS = 8
GRID = 16
SIDE = 4
DEVICES = FRONTS * GRID
FB = 32
TB = FB - LB
TILES = 128
LABEL_ROWS = 4
LABEL_LANES = TILES // LABEL_ROWS
LINES = TB // SIDE
SLICE = BLOCK // SIDE
PSLOTS = LINES * LB
TSLOTS = 88
SLOTS = PSLOTS + TSLOTS
BINS = SIDE * FRONTS * SLOTS
OUT_SLOTS = 2 + LINES
WIDE = 2 * BLOCK
PACKED = [WIDE * (c * (c + 1) // 2) for c in range(LEAD // WIDE + 1)]
SUB = 8
SLABS = BLOCK // SUB
ACCS = 8
VMEM_LIMIT = 60 << 20

highest = lax.Precision.HIGHEST
ANY = pl.BlockSpec(memory_space=pl.ANY)
VMEM = pl.BlockSpec(memory_space=pltpu.VMEM)
SMEM = pl.BlockSpec(memory_space=pltpu.SMEM)


def split(values):
    high = values.astype(jnp.bfloat16)
    return high, (values - high.astype(jnp.float32)).astype(jnp.bfloat16)


def mul(a, b):
    return lax.dot_general(a, b, (((1,), (1,)), ((), ())), preferred_element_type=jnp.float32)


def tdot(a, b):
    return lax.dot_general(
        a, b, (((0,), (0,)), ((), ())), precision=highest, preferred_element_type=jnp.float32
    )


def shift(block, axis, step):
    return lax.ppermute(block, axis, [(i, (i + step) % SIDE) for i in range(SIDE)])


def gather_front(values):
    others = [
        lax.ppermute(values, "front", [(i, i ^ k) for i in range(FRONTS)]) for k in range(1, FRONTS)
    ]
    return jnp.stack([values, *others])


def ring_near(block, axis):
    return shift(block, axis, -1), shift(block, axis, 1)


def ring_far(near, axis):
    from_next, from_prev = near
    half = from_prev.shape[0] // 2
    return shift(from_prev[:half], axis, 1), shift(from_next[half:], axis, -1)


def ring_pieces(block, near, far):
    return [block, near[0], *far, near[1]]


def gather_lines(first, second, given, work):
    lines = []
    for part, axis in ((first, "x"), (second, "y")):
        lines.append(jnp.stack([part, *(shift(part, axis, -n) for n in range(1, SIDE))]))
    lines, given = lax.optimization_barrier((lines, given))
    near = [ring_near(line, axis) for line, axis in zip(lines, ("y", "x"))]
    near, done = lax.optimization_barrier((near, work(given)))
    far = [ring_far(pair, axis) for pair, axis in zip(near, ("y", "x"))]
    return lines, near, far, done


def line_copies(pieces, place, sem, x, y):
    copies = []
    for h in range(2):
        own, nxt, far_a, far_b, prv = pieces[5 * h : 5 * h + 5]
        for outer in range(SIDE):
            for inner in range(SIDE):
                if outer == 2:
                    src = (far_a if inner < 2 else far_b).at[inner % 2]
                else:
                    src = (own, nxt, None, prv)[outer].at[inner]
                dx, dy = (inner, outer) if h == 0 else (outer, inner)
                dst = place(h, (x + dx) % SIDE, (y + dy) % SIDE)
                copies.append(pltpu.make_async_copy(src, dst, sem.at[len(copies)]))
    return copies


def turn_kernel(x, out):
    tiles = out.shape[1]

    def body(i, carry):
        for first in range(0, tiles, SUB):
            rows = x[pl.ds(first * BLOCK + i, SUB, stride=BLOCK), :]
            out[i, first : first + SUB, :] = rows
        return carry

    lax.fori_loop(0, BLOCK, body, 0, unroll=4)


def turn(tiles):
    step = 64
    return pl.pallas_call(
        turn_kernel,
        grid=(TILES // step,),
        out_shape=jax.ShapeDtypeStruct((BLOCK, TILES, BLOCK), jnp.float32),
        in_specs=[pl.BlockSpec((step * BLOCK, BLOCK), lambda n: (n, 0))],
        out_specs=pl.BlockSpec((BLOCK, step, BLOCK), lambda n: (0, n, 0)),
        compiler_params=pltpu.CompilerParams(vmem_limit_bytes=VMEM_LIMIT),
        cost_estimate=pl.CostEstimate(flops=0, bytes_accessed=16 << 20, transcendentals=0),
        name="turn",
    )(tiles.reshape(TILES * BLOCK, BLOCK))


def combine_kernel(position, bins, x, out, *accs):
    sources = x.shape[0] // TILES

    @pl.when(pl.program_id(0) == 0)
    def _():
        for acc in accs:
            acc[...] = jnp.zeros_like(acc)

    def body(q, carry):
        line, k = q // FRONTS, q % FRONTS
        source = line * FRONTS + jnp.bitwise_xor(k, position[2])
        base = pl.multiple_of(source * TILES, TILES)
        labels = (k * GRID + pl.program_id(0) * (sources // FRONTS) + line) * TILES
        for first in range(0, TILES, ACCS):
            at = [bins[labels + first + m] for m in range(ACCS)]
            rows = [x[pl.ds(base + first + m, 1), :] for m in range(ACCS)]
            sums = [accs[m][pl.ds(at[m], 1), :] + rows[m] for m in range(ACCS)]
            for m in range(ACCS):
                accs[m][pl.ds(at[m], 1), :] = sums[m]
        return carry

    lax.fori_loop(0, sources, body, 0)
    step = 256

    @pl.when(pl.program_id(0) == pl.num_programs(0) - 1)
    def _():
        def add(b, carry):
            at = pl.ds(pl.multiple_of(b * step, step), step)
            total = accs[0][at, :]
            for acc in accs[1:]:
                total = total + acc[at, :]
            out[at, :] = total
            return carry

        lax.fori_loop(0, BINS // step, add, 0)


def combine(position, bins, rows):
    steps = 4
    return pl.pallas_call(
        combine_kernel,
        grid=(steps,),
        out_shape=jax.ShapeDtypeStruct((BINS, BLOCK), jnp.float32),
        in_specs=[SMEM, SMEM, pl.BlockSpec((rows.shape[0] // steps, BLOCK), lambda i: (i, 0))],
        out_specs=pl.BlockSpec((BINS, BLOCK), lambda i: (0, 0)),
        scratch_shapes=[pltpu.VMEM((BINS, BLOCK), jnp.float32)] * ACCS,
        compiler_params=pltpu.CompilerParams(vmem_limit_bytes=VMEM_LIMIT),
        cost_estimate=pl.CostEstimate(flops=20 * 10**9, bytes_accessed=20 << 20, transcendentals=0),
        name="combine",
    )(position, bins, rows)


def factor_rows(rows, first, sub):
    def spread(values, j):
        return jnp.broadcast_to(values[j : j + 1, :], values.shape)

    columns = [
        jnp.broadcast_to(rows[:, first + j : first + j + 1], (SUB, BLOCK)) for j in range(SUB)
    ]
    parts = [rows[:, :BLOCK], rows[:, BLOCK:]]
    for j in range(SUB):
        scale = lax.rsqrt(spread(columns[j], j))
        weight = jnp.where(sub > j, columns[j] * scale, 0.0)
        for m in range(j + 1, SUB):
            columns[m] = columns[m] - weight * (spread(columns[m], j) * scale)
        for n in range(2):
            pivot = spread(parts[n], j) * scale
            parts[n] = jnp.where(sub == j, pivot, parts[n] - weight * pivot)
    return jnp.concatenate(parts, 1)


def factor_kernel(position, *refs):
    pieces, outs, scratch = refs[:10], refs[10:13], refs[13:]
    own_rows, inverse, labels = outs
    (entries, work, diag, pair, sem) = scratch
    px, py = position[0], position[1]

    def place(h, x, y):
        block = (x % 2) * SIDE + y
        slab = block * SLABS + (x // 2) * (SLABS // 2) + h * (SLABS // 4)
        return entries.at[pl.ds(slab, SLABS // 4)]

    copies = line_copies(pieces, place, sem, px, py)
    for copy in copies:
        copy.start()
    for copy in copies:
        copy.wait()
    lane = lax.broadcasted_iota(jnp.int32, (1, TILES), 1)
    for g in range(GRID):
        slab = entries[(g % LB) * SLABS + (g // LB) * (SLABS // 2), :, LEAD - TILES :]
        found = jnp.zeros((1, TILES), jnp.float32)
        for n in range(LABEL_ROWS):
            turned = pltpu.roll(slab[n : n + 1], (n + 1) * LABEL_LANES % TILES, 1)
            found = jnp.where(lane // LABEL_LANES == n, turned, found)
        labels[g : g + 1, :] = found.astype(jnp.int32)
    sub = lax.broadcasted_iota(jnp.int32, (SUB, 1), 0)
    row = lax.broadcasted_iota(jnp.int32, (BLOCK, BLOCK), 0)
    col = lax.broadcasted_iota(jnp.int32, (BLOCK, BLOCK), 1)
    eye = jnp.where(row == col, 1.0, 0.0)
    for r in range(LB):
        for c in range(r + 1):
            block = entries[r * SLABS : (r + 1) * SLABS, :, c * BLOCK : (c + 1) * BLOCK]
            block = block.reshape(BLOCK, BLOCK)
            if r == c:
                block = jnp.where(col <= row, block, 0.0)
                block = block + jnp.where(col < row, block, 0.0).T
                work[r * BLOCK : (r + 1) * BLOCK, r * BLOCK : (r + 1) * BLOCK] = block
            else:
                work[c * BLOCK : (c + 1) * BLOCK, r * BLOCK : (r + 1) * BLOCK] = block.T

    def step(k, carry):
        at = pl.ds(pl.multiple_of(k * BLOCK, BLOCK), BLOCK)
        pair[:, :BLOCK] = work[at, at]
        pair[:, BLOCK:] = eye
        for q in range(BLOCK // SUB):
            first = SUB * q
            rows = pair[first : first + SUB, :]
            if q > 0:
                rows = rows - tdot(pair[0:first, first : first + SUB], pair[0:first, :])
            pair[first : first + SUB, :] = factor_rows(rows, first, sub)
        block_inverse = pair[:, BLOCK:]
        diag[k] = pair[:, :BLOCK]
        work[at, :] = jnp.dot(
            block_inverse, work[at, :], precision=highest, preferred_element_type=jnp.float32
        )
        work[at, at] = block_inverse

        def update(i, inner):
            below = pl.ds(pl.multiple_of(i * BLOCK, BLOCK), BLOCK)
            work[below, at] = jnp.zeros((BLOCK, BLOCK), jnp.float32)
            work[below, :] = work[below, :] - tdot(work[at, below], work[at, :])
            return inner

        lax.fori_loop(k + 1, LB, update, 0)
        return carry

    lax.fori_loop(0, LB, step, 0)
    for k in range(LB):
        at = slice(k * BLOCK, (k + 1) * BLOCK)
        start, width = PACKED[k // 2], (k + 1) * BLOCK
        part = slice(k % 2 * BLOCK, (k % 2 + 1) * BLOCK)
        high, low = split(work[at, :width])
        inverse[0, part, start : start + width] = high
        inverse[1, part, start : start + width] = low
        if k % 2 == 0:
            rest = jnp.zeros((2, BLOCK, BLOCK), jnp.bfloat16)
            inverse[:, part, start + width : start + width + BLOCK] = rest
    mine = jnp.minimum(px * SIDE + py, LB - 1)
    mine_at = pl.ds(pl.multiple_of(mine * BLOCK, BLOCK), BLOCK)
    for k in range(LB):
        at = slice(k * BLOCK, (k + 1) * BLOCK)
        block = jnp.where(k == mine, jnp.where(row <= col, diag[k], 0.0), work[at, mine_at])
        own_rows[:, at] = jnp.where(k <= mine, block, 0.0).T


def factor(position, pieces):
    return pl.pallas_call(
        factor_kernel,
        out_shape=[
            jax.ShapeDtypeStruct((BLOCK, LEAD), jnp.float32),
            jax.ShapeDtypeStruct((2, WIDE, PACKED[-1]), jnp.bfloat16),
            jax.ShapeDtypeStruct((GRID, TILES), jnp.int32),
        ],
        in_specs=[SMEM] + [ANY] * 10,
        out_specs=[VMEM] * 3,
        scratch_shapes=[
            pltpu.VMEM((LB * SLABS, SUB, LEAD), jnp.float32),
            pltpu.VMEM((LEAD, LEAD), jnp.float32),
            pltpu.VMEM((LB, BLOCK, BLOCK), jnp.float32),
            pltpu.VMEM((BLOCK, 2 * BLOCK), jnp.float32),
            pltpu.SemaphoreType.DMA((32,)),
        ],
        compiler_params=pltpu.CompilerParams(vmem_limit_bytes=VMEM_LIMIT),
        cost_estimate=pl.CostEstimate(flops=120 * 10**9, bytes_accessed=20 << 20, transcendentals=1024),
        name="factor",
    )(position, *pieces)


def solve_kernel(position, own, part1, part2, part3, sums, inverse, out, rows):
    x = position[0]
    for step, part in enumerate((own, part1, part2, part3)):
        source = (x + SIDE - step) % SIDE
        for l in range(2):
            rows[SIDE * l + source] = part[l]
    for m in range(LINES):
        for c in range(LB):
            at = slice(c * BLOCK, (c + 1) * BLOCK)
            values = sums[pl.ds(m * LB + c, SLICE, stride=SLOTS), :]
            rows[LB // SIDE + m, :, at] = rows[LB // SIDE + m, :, at] + values
    high, low = split(rows[LB // SIDE :].reshape(LINES * SLICE, LEAD))
    for c in range(LEAD // WIDE):
        end = (c + 1) * WIDE
        inv_high, inv_low = inverse[:, :, PACKED[c] : PACKED[c + 1]]
        value = mul(high[:, :end], inv_high) + (
            mul(high[:, :end], inv_low) + mul(low[:, :end], inv_high)
        )
        out[:, :, end - WIDE : end] = value.reshape(LINES, SLICE, WIDE)


def solve(position, parts, sums, inverse):
    return pl.pallas_call(
        solve_kernel,
        out_shape=jax.ShapeDtypeStruct((LINES, SLICE, LEAD), jnp.float32),
        in_specs=[SMEM] + [VMEM] * 6,
        out_specs=VMEM,
        scratch_shapes=[pltpu.VMEM((2 * SIDE, SLICE, LEAD), jnp.float32)],
        compiler_params=pltpu.CompilerParams(vmem_limit_bytes=20 << 20),
        name="solve",
    )(position, *parts, sums, inverse)


def product_kernel(position, *refs):
    along_x, along_y, scratch = refs[:5], refs[5:10], refs[10:]
    sums, out, own, high, low, row_high, row_low = scratch
    x, y = position[0], position[1]
    half = LINES // 2
    out[...] = jnp.zeros_like(out)

    def blocks(pieces, here):
        nearby, nxt, far_a, far_b, prv = pieces
        for step, piece, first in (
            (0, nearby, 0),
            (1, nxt, 0),
            (2, far_a, 0),
            (2, far_b, half),
            (3, prv, 0),
        ):
            for m in range(piece.shape[0]):
                yield (here + step) % SIDE, first + m, piece[m]

    for index, m, values in blocks(along_x, x):
        at = pl.ds(pl.multiple_of(m * BLOCK + index * SLICE, SLICE), SLICE)
        high[at, :], low[at, :] = split(values)
    for l in range(2):
        m = jnp.maximum(x - 2, 0) if l == 0 else x + 2
        nearby, nxt, far_a, far_b, prv = along_x
        for step in range(SIDE):
            at = pl.ds(pl.multiple_of((x + step) % SIDE * SLICE, SLICE), SLICE)
            if step == 2:
                first = far_a[jnp.minimum(m, half - 1)]
                second = far_b[jnp.maximum(m - half, 0)]
                own[l, at, :] = jnp.where(m < half, first, second)
            else:
                own[l, at, :] = (nearby, nxt, None, prv)[step][m]
    for z, m, values in blocks(along_y, y):
        at = pl.ds(pl.multiple_of(m * BLOCK + z * SLICE, SLICE), SLICE)
        row_high[at, :], row_low[at, :] = split(values)
    for pair in range(LINES // 2):
        start = pair * 2 * BLOCK
        rows_high, rows_low = row_high[start:], row_low[start:]
        cols_high, cols_low = high[start : start + 2 * BLOCK], low[start : start + 2 * BLOCK]
        value = mul(rows_high, cols_high) + (mul(rows_high, cols_low) + mul(rows_low, cols_high))
        for row_block in range(LB + 2 * pair * SIDE, FB):
            owner, first = row_block % GRID, 2 if row_block >= GRID else 0
            line = (row_block - LB) * SLICE - start
            for n in range(2 * pair, 2 * pair + 2):
                if first + n >= OUT_SLOTS or (first == 0 and n >= 2):
                    continue
                below = jnp.maximum(row_block - LB - y - SIDE * n, 0)
                slot = (TB - y) * n - 2 * n * (n - 1) + below
                tiles = sums[pl.ds(PSLOTS + slot, SLICE, stride=SLOTS), :]
                col = (n - 2 * pair) * BLOCK
                out[owner, first + n] = tiles - value[line : line + SLICE, col : col + BLOCK]


def product(position, along_x, along_y, sums):
    return pl.pallas_call(
        product_kernel,
        out_shape=[
            jax.ShapeDtypeStruct((GRID, OUT_SLOTS, SLICE, BLOCK), jnp.float32),
            jax.ShapeDtypeStruct((2, BLOCK, LEAD), jnp.float32),
        ],
        in_specs=[SMEM] + [VMEM] * 11,
        out_specs=[VMEM] * 2,
        scratch_shapes=[
            pltpu.VMEM((LINES * BLOCK, LEAD), jnp.bfloat16),
            pltpu.VMEM((LINES * BLOCK, LEAD), jnp.bfloat16),
            pltpu.VMEM((LINES * BLOCK, LEAD), jnp.bfloat16),
            pltpu.VMEM((LINES * BLOCK, LEAD), jnp.bfloat16),
        ],
        compiler_params=pltpu.CompilerParams(vmem_limit_bytes=32 << 20),
        cost_estimate=pl.CostEstimate(flops=11 * 10**9, bytes_accessed=8 << 20, transcendentals=0),
        name="product",
    )(position, *along_x, *along_y, sums)


def lower(values, row_block, block, first_row):
    row = lax.broadcasted_iota(jnp.int32, values.shape, 0)
    col = lax.broadcasted_iota(jnp.int32, values.shape, 1)
    inside = block * BLOCK + col <= row_block * BLOCK + first_row + row
    return jnp.where(inside, values, 0.0)


def base_kernel(position, lead_rows, own, out):
    g = position[0] * SIDE + position[1]
    out[0, :, :LEAD] = jnp.where(g < LB, lead_rows[...], own[0])
    out[1, :, :LEAD] = own[1]
    out[:, :, LEAD:] = jnp.zeros((2, BLOCK, TB * BLOCK), jnp.float32)


def base(position, shape, lead_rows, own):
    return pl.pallas_call(
        base_kernel,
        out_shape=jax.ShapeDtypeStruct(shape, jnp.float32),
        in_specs=[SMEM, VMEM, VMEM],
        out_specs=VMEM,
        compiler_params=pltpu.CompilerParams(vmem_limit_bytes=16 << 20),
        cost_estimate=pl.CostEstimate(flops=0, bytes_accessed=32 << 20, transcendentals=0),
        name="base",
    )(position, lead_rows, own)


def finish_kernel(position, before, entries_in, change_in, out, entries, change, values, sem):
    g = position[0] * SIDE + position[1]
    wide = SIDE * BLOCK
    steps = [(0, n) for n in range(2)] + [(1, n) for n in range(LINES)]
    arriving, leaving = [], []
    for i, (local, n) in enumerate(steps):
        at = pl.ds(LEAD + n * wide, wide)
        arriving.append(
            (
                pltpu.make_async_copy(entries_in.at[local, :, at], entries.at[i], sem.at[0, i]),
                pltpu.make_async_copy(change_in.at[:, i], change.at[i], sem.at[1, i]),
            )
        )
        leaving.append(pltpu.make_async_copy(values.at[i], out.at[local, :, at], sem.at[2, i]))
    for pair in arriving:
        for copy in pair:
            copy.start()
    for i, (local, n) in enumerate(steps):
        for copy in arriving[i]:
            copy.wait()
        for y in range(SIDE):
            at = slice(y * BLOCK, (y + 1) * BLOCK)
            for x in range(SIDE):
                span = slice(x * SLICE, (x + 1) * SLICE)
                value = entries[i, span, at] + change[i, x * SIDE + y]
                block = LB + n * SIDE + y
                values[i, span, at] = lower(value, local * GRID + g, block, x * SLICE)
        leaving[i].start()
    for copy in leaving:
        copy.wait()


def finish(position, before, entries, change):
    return pl.pallas_call(
        finish_kernel,
        out_shape=jax.ShapeDtypeStruct(before.shape, jnp.float32),
        in_specs=[SMEM, ANY, ANY, ANY],
        out_specs=ANY,
        input_output_aliases={1: 0},
        scratch_shapes=[
            pltpu.VMEM((OUT_SLOTS, BLOCK, SIDE * BLOCK), jnp.float32),
            pltpu.VMEM((OUT_SLOTS, GRID, SLICE, BLOCK), jnp.float32),
            pltpu.VMEM((OUT_SLOTS, BLOCK, SIDE * BLOCK), jnp.float32),
            pltpu.SemaphoreType.DMA((3, OUT_SLOTS)),
        ],
        compiler_params=pltpu.CompilerParams(vmem_limit_bytes=VMEM_LIMIT),
        name="finish",
    )(position, before, entries, change)


def destination_bins(owners, local_rows, picks):
    front, g = owners // GRID, owners % GRID
    shifted = local_rows + (local_rows * GRID + g < LB).astype(jnp.int32)
    row_block = shifted * GRID + g
    col_block = picks % (row_block + 1)
    panel = (row_block % SIDE * FRONTS + front) * SLOTS + (row_block - LB) // SIDE * LB + col_block
    y, n = col_block % SIDE, (col_block - LB) // SIDE
    slot = (TB - y) * n - 2 * n * (n - 1) + row_block - col_block
    trail = (y * FRONTS + front) * SLOTS + PSLOTS + slot
    return jnp.where(col_block < LB, panel, trail)


def across(values, axes):
    return lax.all_to_all(values, axes, split_axis=0, concat_axis=0)


def local(front_entries, child_tiles, tile_owner, tile_rows, tile_picks):
    x, y, f = lax.axis_index("x"), lax.axis_index("y"), lax.axis_index("front")
    position = jnp.stack([x, y, f]).astype(jnp.int32)
    entries = front_entries[0, :, 0]
    half = BLOCK // 2
    lead = entries[0, :, :LEAD]
    other = lax.ppermute(lead[half:], "x", [(0, 2), (1, 3)])
    lead = jnp.where(x < 2, lead[:half], other)
    bins = destination_bins(tile_owner[0, :, 0], tile_rows[0], tile_picks[0])
    bins = bins.astype(jnp.float32).reshape(LABEL_ROWS, LABEL_LANES)
    lead = lax.dynamic_update_slice(lead, bins, (0, LEAD - LABEL_LANES))
    lead, tiles = lax.optimization_barrier((lead.reshape(SLABS // 2, SUB, LEAD), child_tiles))
    half = SLABS // 4
    lines, near, far, tiles = gather_lines(
        lead[:half], lead[half:], tiles, turn
    )
    tiles, near, entries = lax.optimization_barrier((tiles, near, entries))
    lead = [piece for ring in zip(lines, near, far) for piece in ring_pieces(*ring)]
    rows = across(tiles, ("x", "y", "front")).reshape(-1, BLOCK)
    panel = entries[:, :, :LEAD].reshape(2, SIDE, SLICE, LEAD)
    panel = [
        lax.dynamic_index_in_dim(panel, (x + n) % SIDE, 1, keepdims=False) for n in range(SIDE)
    ]
    panel = [part if n == 0 else shift(part, "x", n) for n, part in enumerate(panel)]
    lead_rows, inverse, bins = factor(position, lead)
    bins = gather_front(bins).reshape(-1)
    sums = combine(position, bins, rows).reshape(SLICE, SLOTS, BLOCK)
    sums = across(sums, ("y", "front")).reshape(-1, BLOCK)
    solved = solve(position, panel, sums, inverse)
    near = [ring_near(solved, axis) for axis in ("x", "y")]
    far = [ring_far(pair, axis) for pair, axis in zip(near, ("x", "y"))]
    along = [ring_pieces(solved, *pair) for pair in zip(near, far)]
    change, own = product(position, *along, sums)
    change = across(change, ("x", "y"))
    out = finish(position, base(position, entries.shape, lead_rows, own), entries, change)
    return out[None, :, None]


def solution(mesh):
    mesh = Mesh(mesh.devices.reshape(FRONTS, SIDE, SIDE), ("front", "x", "y"))
    grid = ("x", "y")
    return jax.shard_map(
        local,
        mesh=mesh,
        in_specs=(
            P("front", None, grid, None, None),
            P("front", grid, None, None),
            P("front", grid, None),
            P("front", grid),
            P("front", grid),
        ),
        out_specs=P("front", None, grid, None, None),
        check_vma=False,
    )
```

```python
import functools
import jax
import jax.numpy as jnp
from jax import lax
from jax.experimental import pallas as pl
from jax.experimental.pallas import tpu as pltpu
from jax.sharding import Mesh
from jax.sharding import PartitionSpec as P

BLOCK = 128
LEAD = 1024
LB = LEAD // BLOCK
FRONTS = 8
GRID = 16
SIDE = 4
DEVICES = FRONTS * GRID
FB = 32
TB = FB - LB
TILES = 128
LABEL_ROWS = 4
LABEL_LANES = TILES // LABEL_ROWS
LINES = TB // SIDE
SLICE = BLOCK // SIDE
PSLOTS = LINES * LB
TSLOTS = 88
SLOTS = PSLOTS + TSLOTS
BINS = SIDE * FRONTS * SLOTS
OUT_SLOTS = 2 + LINES
WIDE = 2 * BLOCK
PACKED = [WIDE * (c * (c + 1) // 2) for c in range(LEAD // WIDE + 1)]
SUB = 8
SLABS = BLOCK // SUB
ACCS = 8
VMEM_LIMIT = 60 << 20

highest = lax.Precision.HIGHEST
ANY = pl.BlockSpec(memory_space=pl.ANY)
VMEM = pl.BlockSpec(memory_space=pltpu.VMEM)
SMEM = pl.BlockSpec(memory_space=pltpu.SMEM)


def split(values):
    high = values.astype(jnp.bfloat16)
    return high, (values - high.astype(jnp.float32)).astype(jnp.bfloat16)


def mul(a, b):
    return lax.dot_general(a, b, (((1,), (1,)), ((), ())), preferred_element_type=jnp.float32)


def tdot(a, b):
    return lax.dot_general(
        a, b, (((0,), (0,)), ((), ())), precision=highest, preferred_element_type=jnp.float32
    )


def shift(block, axis, step):
    return lax.ppermute(block, axis, [(i, (i + step) % SIDE) for i in range(SIDE)])


def gather_front(values):
    others = [
        lax.ppermute(values, "front", [(i, i ^ k) for i in range(FRONTS)]) for k in range(1, FRONTS)
    ]
    return jnp.stack([values, *others])


def ring_near(block, axis):
    return shift(block, axis, -1), shift(block, axis, 1)


def ring_far(near, axis):
    from_next, from_prev = near
    half = from_prev.shape[0] // 2
    return shift(from_prev[:half], axis, 1), shift(from_next[half:], axis, -1)


def ring_pieces(block, near, far):
    return [block, near[0], *far, near[1]]


def gather_lines(first, second, given, work):
    lines = []
    for part, axis in ((first, "x"), (second, "y")):
        lines.append(jnp.stack([part, *(shift(part, axis, -n) for n in range(1, SIDE))]))
    lines, given = lax.optimization_barrier((lines, given))
    near = [ring_near(line, axis) for line, axis in zip(lines, ("y", "x"))]
    near, done = lax.optimization_barrier((near, work(given)))
    far = [ring_far(pair, axis) for pair, axis in zip(near, ("y", "x"))]
    return lines, near, far, done


def line_copies(pieces, place, sem, x, y):
    copies = []
    for h in range(2):
        own, nxt, far_a, far_b, prv = pieces[5 * h : 5 * h + 5]
        for outer in range(SIDE):
            for inner in range(SIDE):
                if outer == 2:
                    src = (far_a if inner < 2 else far_b).at[inner % 2]
                else:
                    src = (own, nxt, None, prv)[outer].at[inner]
                dx, dy = (inner, outer) if h == 0 else (outer, inner)
                dst = place(h, (x + dx) % SIDE, (y + dy) % SIDE)
                copies.append(pltpu.make_async_copy(src, dst, sem.at[len(copies)]))
    return copies


def turn_kernel(x, out):
    tiles = out.shape[1]

    def body(i, carry):
        for first in range(0, tiles, SUB):
            rows = x[pl.ds(first * BLOCK + i, SUB, stride=BLOCK), :]
            out[i, first : first + SUB, :] = rows
        return carry

    lax.fori_loop(0, BLOCK, body, 0, unroll=4)


def turn(tiles):
    step = 32
    return pl.pallas_call(
        turn_kernel,
        grid=(TILES // step,),
        out_shape=jax.ShapeDtypeStruct((BLOCK, TILES, BLOCK), jnp.float32),
        in_specs=[pl.BlockSpec((step * BLOCK, BLOCK), lambda n: (n, 0))],
        out_specs=pl.BlockSpec((BLOCK, step, BLOCK), lambda n: (0, n, 0)),
        compiler_params=pltpu.CompilerParams(vmem_limit_bytes=VMEM_LIMIT),
        cost_estimate=pl.CostEstimate(flops=0, bytes_accessed=16 << 20, transcendentals=0),
        name="turn",
    )(tiles.reshape(TILES * BLOCK, BLOCK))


def combine_kernel(position, bins, x, out, *accs):
    sources = x.shape[0] // TILES

    @pl.when(pl.program_id(0) == 0)
    def _():
        for acc in accs:
            acc[...] = jnp.zeros_like(acc)

    def body(q, carry):
        line, k = q // FRONTS, q % FRONTS
        source = line * FRONTS + jnp.bitwise_xor(k, position[2])
        base = pl.multiple_of(source * TILES, TILES)
        labels = (k * GRID + pl.program_id(0) * (sources // FRONTS) + line) * TILES
        for first in range(0, TILES, ACCS):
            at = [bins[labels + first + m] for m in range(ACCS)]
            rows = [x[pl.ds(base + first + m, 1), :] for m in range(ACCS)]
            sums = [accs[m][pl.ds(at[m], 1), :] + rows[m] for m in range(ACCS)]
            for m in range(ACCS):
                accs[m][pl.ds(at[m], 1), :] = sums[m]
        return carry

    lax.fori_loop(0, sources, body, 0)
    step = 256

    @pl.when(pl.program_id(0) == pl.num_programs(0) - 1)
    def _():
        def add(b, carry):
            at = pl.ds(pl.multiple_of(b * step, step), step)
            total = accs[0][at, :]
            for acc in accs[1:]:
                total = total + acc[at, :]
            out[at, :] = total
            return carry

        lax.fori_loop(0, BINS // step, add, 0)


def combine(position, bins, rows):
    steps = 4
    return pl.pallas_call(
        combine_kernel,
        grid=(steps,),
        out_shape=jax.ShapeDtypeStruct((BINS, BLOCK), jnp.float32),
        in_specs=[SMEM, SMEM, pl.BlockSpec((rows.shape[0] // steps, BLOCK), lambda i: (i, 0))],
        out_specs=pl.BlockSpec((BINS, BLOCK), lambda i: (0, 0)),
        scratch_shapes=[pltpu.VMEM((BINS, BLOCK), jnp.float32)] * ACCS,
        compiler_params=pltpu.CompilerParams(vmem_limit_bytes=VMEM_LIMIT),
        cost_estimate=pl.CostEstimate(flops=20 * 10**9, bytes_accessed=20 << 20, transcendentals=0),
        name="combine",
    )(position, bins, rows)


def factor_rows(rows, first, sub):
    def spread(values, j):
        return jnp.broadcast_to(values[j : j + 1, :], values.shape)

    columns = [
        jnp.broadcast_to(rows[:, first + j : first + j + 1], (SUB, BLOCK)) for j in range(SUB)
    ]
    parts = [rows[:, :BLOCK], rows[:, BLOCK:]]
    for j in range(SUB):
        scale = lax.rsqrt(spread(columns[j], j))
        weight = jnp.where(sub > j, columns[j] * scale, 0.0)
        for m in range(j + 1, SUB):
            columns[m] = columns[m] - weight * (spread(columns[m], j) * scale)
        for n in range(2):
            pivot = spread(parts[n], j) * scale
            parts[n] = jnp.where(sub == j, pivot, parts[n] - weight * pivot)
    return jnp.concatenate(parts, 1)


def factor_kernel(position, *refs):
    pieces, outs, scratch = refs[:10], refs[10:13], refs[13:]
    own_rows, inverse, labels = outs
    (entries, work, diag, pair, sem) = scratch
    px, py = position[0], position[1]

    def place(h, x, y):
        block = (x % 2) * SIDE + y
        slab = block * SLABS + (x // 2) * (SLABS // 2) + h * (SLABS // 4)
        return entries.at[pl.ds(slab, SLABS // 4)]

    copies = line_copies(pieces, place, sem, px, py)
    for copy in copies:
        copy.start()
    for copy in copies:
        copy.wait()
    lane = lax.broadcasted_iota(jnp.int32, (1, TILES), 1)
    for g in range(GRID):
        slab = entries[(g % LB) * SLABS + (g // LB) * (SLABS // 2), :, LEAD - TILES :]
        found = jnp.zeros((1, TILES), jnp.float32)
        for n in range(LABEL_ROWS):
            turned = pltpu.roll(slab[n : n + 1], (n + 1) * LABEL_LANES % TILES, 1)
            found = jnp.where(lane // LABEL_LANES == n, turned, found)
        labels[g : g + 1, :] = found.astype(jnp.int32)
    sub = lax.broadcasted_iota(jnp.int32, (SUB, 1), 0)
    row = lax.broadcasted_iota(jnp.int32, (BLOCK, BLOCK), 0)
    col = lax.broadcasted_iota(jnp.int32, (BLOCK, BLOCK), 1)
    eye = jnp.where(row == col, 1.0, 0.0)
    for r in range(LB):
        for c in range(r + 1):
            block = entries[r * SLABS : (r + 1) * SLABS, :, c * BLOCK : (c + 1) * BLOCK]
            block = block.reshape(BLOCK, BLOCK)
            if r == c:
                block = jnp.where(col <= row, block, 0.0)
                block = block + jnp.where(col < row, block, 0.0).T
                work[r * BLOCK : (r + 1) * BLOCK, r * BLOCK : (r + 1) * BLOCK] = block
            else:
                work[c * BLOCK : (c + 1) * BLOCK, r * BLOCK : (r + 1) * BLOCK] = block.T

    def step(k, carry):
        at = pl.ds(pl.multiple_of(k * BLOCK, BLOCK), BLOCK)
        pair[:, :BLOCK] = work[at, at]
        pair[:, BLOCK:] = eye
        for q in range(BLOCK // SUB):
            first = SUB * q
            rows = pair[first : first + SUB, :]
            if q > 0:
                rows = rows - tdot(pair[0:first, first : first + SUB], pair[0:first, :])
            pair[first : first + SUB, :] = factor_rows(rows, first, sub)
        block_inverse = pair[:, BLOCK:]
        diag[k] = pair[:, :BLOCK]
        work[at, :] = jnp.dot(
            block_inverse, work[at, :], precision=highest, preferred_element_type=jnp.float32
        )
        work[at, at] = block_inverse

        def update(i, inner):
            below = pl.ds(pl.multiple_of(i * BLOCK, BLOCK), BLOCK)
            work[below, at] = jnp.zeros((BLOCK, BLOCK), jnp.float32)
            work[below, :] = work[below, :] - tdot(work[at, below], work[at, :])
            return inner

        lax.fori_loop(k + 1, LB, update, 0)
        return carry

    lax.fori_loop(0, LB, step, 0)
    for k in range(LB):
        at = slice(k * BLOCK, (k + 1) * BLOCK)
        start, width = PACKED[k // 2], (k + 1) * BLOCK
        part = slice(k % 2 * BLOCK, (k % 2 + 1) * BLOCK)
        high, low = split(work[at, :width])
        inverse[0, part, start : start + width] = high
        inverse[1, part, start : start + width] = low
        if k % 2 == 0:
            rest = jnp.zeros((2, BLOCK, BLOCK), jnp.bfloat16)
            inverse[:, part, start + width : start + width + BLOCK] = rest
    mine = jnp.minimum(px * SIDE + py, LB - 1)
    mine_at = pl.ds(pl.multiple_of(mine * BLOCK, BLOCK), BLOCK)
    for k in range(LB):
        at = slice(k * BLOCK, (k + 1) * BLOCK)
        block = jnp.where(k == mine, jnp.where(row <= col, diag[k], 0.0), work[at, mine_at])
        own_rows[:, at] = jnp.where(k <= mine, block, 0.0).T


def factor(position, pieces):
    return pl.pallas_call(
        factor_kernel,
        out_shape=[
            jax.ShapeDtypeStruct((BLOCK, LEAD), jnp.float32),
            jax.ShapeDtypeStruct((2, WIDE, PACKED[-1]), jnp.bfloat16),
            jax.ShapeDtypeStruct((GRID, TILES), jnp.int32),
        ],
        in_specs=[SMEM] + [ANY] * 10,
        out_specs=[VMEM] * 3,
        scratch_shapes=[
            pltpu.VMEM((LB * SLABS, SUB, LEAD), jnp.float32),
            pltpu.VMEM((LEAD, LEAD), jnp.float32),
            pltpu.VMEM((LB, BLOCK, BLOCK), jnp.float32),
            pltpu.VMEM((BLOCK, 2 * BLOCK), jnp.float32),
            pltpu.SemaphoreType.DMA((32,)),
        ],
        compiler_params=pltpu.CompilerParams(vmem_limit_bytes=VMEM_LIMIT),
        cost_estimate=pl.CostEstimate(flops=120 * 10**9, bytes_accessed=20 << 20, transcendentals=1024),
        name="factor",
    )(position, *pieces)


def solve_kernel(position, own, part1, part2, part3, sums, inverse, first, second, rows):
    x = position[0]
    for step, part in enumerate((own, part1, part2, part3)):
        source = (x + SIDE - step) % SIDE
        for l in range(2):
            rows[SIDE * l + source] = part[l]
    for m in range(LINES):
        for c in range(LB):
            at = slice(c * BLOCK, (c + 1) * BLOCK)
            values = sums[pl.ds(m * LB + c, SLICE, stride=SLOTS), :]
            rows[LB // SIDE + m, :, at] = rows[LB // SIDE + m, :, at] + values
    high, low = split(rows[LB // SIDE :].reshape(LINES * SLICE, LEAD))
    for c in range(LEAD // WIDE):
        end = (c + 1) * WIDE
        inv_high, inv_low = inverse[:, :, PACKED[c] : PACKED[c + 1]]
        value = mul(high[:, :end], inv_high) + (
            mul(high[:, :end], inv_low) + mul(low[:, :end], inv_high)
        )
        value = value.reshape(2, LINES // 2, SLICE, WIDE)
        first[:, :, end - WIDE : end] = value[0]
        second[:, :, end - WIDE : end] = value[1]


def solve(position, parts, sums, inverse):
    return pl.pallas_call(
        solve_kernel,
        out_shape=[jax.ShapeDtypeStruct((LINES // 2, SLICE, LEAD), jnp.float32)] * 2,
        in_specs=[SMEM] + [VMEM] * 6,
        out_specs=[VMEM] * 2,
        scratch_shapes=[pltpu.VMEM((2 * SIDE, SLICE, LEAD), jnp.float32)],
        compiler_params=pltpu.CompilerParams(vmem_limit_bytes=20 << 20),
        name="solve",
    )(position, *parts, sums, inverse)


def product_kernel(position, *refs):
    along_x, along_y, scratch = refs[:8], refs[8:16], refs[16:]
    sums, out, own, high, low, row_high, row_low = scratch
    x, y = position[0], position[1]
    half = LINES // 2
    out[...] = jnp.zeros_like(out)

    def blocks(pieces, here):
        for n, piece in enumerate(pieces):
            for m in range(half):
                yield (here + n // 2) % SIDE, n % 2 * half + m, piece[m]

    for index, m, values in blocks(along_x, x):
        at = pl.ds(pl.multiple_of(m * BLOCK + index * SLICE, SLICE), SLICE)
        high[at, :], low[at, :] = split(values)
    for l in range(2):
        m = jnp.maximum(x - 2, 0) if l == 0 else x + 2
        for step in range(SIDE):
            at = pl.ds(pl.multiple_of((x + step) % SIDE * SLICE, SLICE), SLICE)
            first = along_x[2 * step][jnp.minimum(m, half - 1)]
            second = along_x[2 * step + 1][jnp.maximum(m - half, 0)]
            own[l, at, :] = jnp.where(m < half, first, second)
    for z, m, values in blocks(along_y, y):
        at = pl.ds(pl.multiple_of(m * BLOCK + z * SLICE, SLICE), SLICE)
        row_high[at, :], row_low[at, :] = split(values)
    for pair in range(LINES // 2):
        start = pair * 2 * BLOCK
        rows_high, rows_low = row_high[start:], row_low[start:]
        cols_high, cols_low = high[start : start + 2 * BLOCK], low[start : start + 2 * BLOCK]
        value = mul(rows_high, cols_high) + (mul(rows_high, cols_low) + mul(rows_low, cols_high))
        for row_block in range(LB + 2 * pair * SIDE, FB):
            owner, first = row_block % GRID, 2 if row_block >= GRID else 0
            line = (row_block - LB) * SLICE - start
            for n in range(2 * pair, 2 * pair + 2):
                if first + n >= OUT_SLOTS or (first == 0 and n >= 2):
                    continue
                below = jnp.maximum(row_block - LB - y - SIDE * n, 0)
                slot = (TB - y) * n - 2 * n * (n - 1) + below
                tiles = sums[pl.ds(PSLOTS + slot, SLICE, stride=SLOTS), :]
                col = (n - 2 * pair) * BLOCK
                out[owner, first + n] = tiles - value[line : line + SLICE, col : col + BLOCK]


def product(position, along_x, along_y, sums):
    return pl.pallas_call(
        product_kernel,
        out_shape=[
            jax.ShapeDtypeStruct((GRID, OUT_SLOTS, SLICE, BLOCK), jnp.float32),
            jax.ShapeDtypeStruct((2, BLOCK, LEAD), jnp.float32),
        ],
        in_specs=[SMEM] + [VMEM] * 17,
        out_specs=[VMEM] * 2,
        scratch_shapes=[
            pltpu.VMEM((LINES * BLOCK, LEAD), jnp.bfloat16),
            pltpu.VMEM((LINES * BLOCK, LEAD), jnp.bfloat16),
            pltpu.VMEM((LINES * BLOCK, LEAD), jnp.bfloat16),
            pltpu.VMEM((LINES * BLOCK, LEAD), jnp.bfloat16),
        ],
        compiler_params=pltpu.CompilerParams(vmem_limit_bytes=32 << 20),
        cost_estimate=pl.CostEstimate(flops=11 * 10**9, bytes_accessed=8 << 20, transcendentals=0),
        name="product",
    )(position, *along_x, *along_y, sums)


def lower(values, row_block, block, first_row):
    row = lax.broadcasted_iota(jnp.int32, values.shape, 0)
    col = lax.broadcasted_iota(jnp.int32, values.shape, 1)
    inside = block * BLOCK + col <= row_block * BLOCK + first_row + row
    return jnp.where(inside, values, 0.0)


def base_kernel(position, lead_rows, own, out):
    g = position[0] * SIDE + position[1]
    out[0, :, :LEAD] = jnp.where(g < LB, lead_rows[...], own[0])
    out[1, :, :LEAD] = own[1]
    out[:, :, LEAD:] = jnp.zeros((2, BLOCK, TB * BLOCK), jnp.float32)


def base(position, shape, lead_rows, own):
    return pl.pallas_call(
        base_kernel,
        out_shape=jax.ShapeDtypeStruct(shape, jnp.float32),
        in_specs=[SMEM, VMEM, VMEM],
        out_specs=VMEM,
        compiler_params=pltpu.CompilerParams(vmem_limit_bytes=16 << 20),
        cost_estimate=pl.CostEstimate(flops=0, bytes_accessed=32 << 20, transcendentals=0),
        name="base",
    )(position, lead_rows, own)


def finish_kernel(position, before, entries_in, change_in, out, entries, change, values, sem):
    g = position[0] * SIDE + position[1]
    wide = SIDE * BLOCK
    steps = [(0, n) for n in range(2)] + [(1, n) for n in range(LINES)]
    arriving, leaving = [], []
    for i, (local, n) in enumerate(steps):
        at = pl.ds(LEAD + n * wide, wide)
        arriving.append(
            (
                pltpu.make_async_copy(entries_in.at[local, :, at], entries.at[i], sem.at[0, i]),
                pltpu.make_async_copy(change_in.at[:, i], change.at[i], sem.at[1, i]),
            )
        )
        leaving.append(pltpu.make_async_copy(values.at[i], out.at[local, :, at], sem.at[2, i]))
    for pair in arriving:
        for copy in pair:
            copy.start()
    for i, (local, n) in enumerate(steps):
        for copy in arriving[i]:
            copy.wait()
        for y in range(SIDE):
            at = slice(y * BLOCK, (y + 1) * BLOCK)
            for x in range(SIDE):
                span = slice(x * SLICE, (x + 1) * SLICE)
                value = entries[i, span, at] + change[i, x * SIDE + y]
                block = LB + n * SIDE + y
                values[i, span, at] = lower(value, local * GRID + g, block, x * SLICE)
        leaving[i].start()
    for copy in leaving:
        copy.wait()


def finish(position, before, entries, change):
    return pl.pallas_call(
        finish_kernel,
        out_shape=jax.ShapeDtypeStruct(before.shape, jnp.float32),
        in_specs=[SMEM, ANY, ANY, ANY],
        out_specs=ANY,
        input_output_aliases={1: 0},
        scratch_shapes=[
            pltpu.VMEM((OUT_SLOTS, BLOCK, SIDE * BLOCK), jnp.float32),
            pltpu.VMEM((OUT_SLOTS, GRID, SLICE, BLOCK), jnp.float32),
            pltpu.VMEM((OUT_SLOTS, BLOCK, SIDE * BLOCK), jnp.float32),
            pltpu.SemaphoreType.DMA((3, OUT_SLOTS)),
        ],
        compiler_params=pltpu.CompilerParams(vmem_limit_bytes=VMEM_LIMIT),
        name="finish",
    )(position, before, entries, change)


def destination_bins(owners, local_rows, picks):
    front, g = owners // GRID, owners % GRID
    shifted = local_rows + (local_rows * GRID + g < LB).astype(jnp.int32)
    row_block = shifted * GRID + g
    col_block = picks % (row_block + 1)
    panel = (row_block % SIDE * FRONTS + front) * SLOTS + (row_block - LB) // SIDE * LB + col_block
    y, n = col_block % SIDE, (col_block - LB) // SIDE
    slot = (TB - y) * n - 2 * n * (n - 1) + row_block - col_block
    trail = (y * FRONTS + front) * SLOTS + PSLOTS + slot
    return jnp.where(col_block < LB, panel, trail)


def across(values, axes):
    return lax.all_to_all(values, axes, split_axis=0, concat_axis=0)


def local(front_entries, child_tiles, tile_owner, tile_rows, tile_picks):
    x, y, f = lax.axis_index("x"), lax.axis_index("y"), lax.axis_index("front")
    position = jnp.stack([x, y, f]).astype(jnp.int32)
    entries = front_entries[0, :, 0]
    half = BLOCK // 2
    lead = entries[0, :, :LEAD]
    other = lax.ppermute(lead[half:], "x", [(0, 2), (1, 3)])
    lead = jnp.where(x < 2, lead[:half], other)
    bins = destination_bins(tile_owner[0, :, 0], tile_rows[0], tile_picks[0])
    bins = bins.astype(jnp.float32).reshape(LABEL_ROWS, LABEL_LANES)
    lead = lax.dynamic_update_slice(lead, bins, (0, LEAD - LABEL_LANES))
    lead, tiles = lax.optimization_barrier((lead.reshape(SLABS // 2, SUB, LEAD), child_tiles))
    half = SLABS // 4
    lines, near, far, tiles = gather_lines(
        lead[:half], lead[half:], tiles, turn
    )
    tiles, near, entries = lax.optimization_barrier((tiles, near, entries))
    lead = [piece for ring in zip(lines, near, far) for piece in ring_pieces(*ring)]
    rows = across(tiles, ("x", "y", "front")).reshape(-1, BLOCK)
    panel = entries[:, :, :LEAD].reshape(2, SIDE, SLICE, LEAD)
    panel = [
        lax.dynamic_index_in_dim(panel, (x + n) % SIDE, 1, keepdims=False) for n in range(SIDE)
    ]
    panel = [part if n == 0 else shift(part, "x", n) for n, part in enumerate(panel)]
    lead_rows, inverse, bins = factor(position, lead)
    bins = gather_front(bins).reshape(-1)
    sums = combine(position, bins, rows).reshape(SLICE, SLOTS, BLOCK)
    sums = across(sums, ("y", "front")).reshape(-1, BLOCK)
    solved = solve(position, panel, sums, inverse)
    along = []
    for axis in ("x", "y"):
        nxt = [shift(part, axis, -1) for part in solved]
        prv = [shift(part, axis, 1) for part in solved]
        far = [shift(prv[0], axis, 1), shift(nxt[1], axis, -1)]
        along.append([*solved, *nxt, *far, *prv])
    change, own = product(position, *along, sums)
    change = across(change, ("x", "y"))
    out = finish(position, base(position, entries.shape, lead_rows, own), entries, change)
    return out[None, :, None]


def solution(mesh):
    mesh = Mesh(mesh.devices.reshape(FRONTS, SIDE, SIDE), ("front", "x", "y"))
    grid = ("x", "y")
    return jax.shard_map(
        local,
        mesh=mesh,
        in_specs=(
            P("front", None, grid, None, None),
            P("front", grid, None, None),
            P("front", grid, None),
            P("front", grid),
            P("front", grid),
        ),
        out_specs=P("front", None, grid, None, None),
        check_vma=False,
    )
```
